256 devices in a mesh: dom: 64 (over z, y, core), quad: 4 (over x).
Axes of the slice: x: 4, y: 4, z: 8, core: 2. Of those that a mesh axis runs over, the one named last changes fastest.
Arguments:
- element_dofs: float32 [56, 9, 65536], P(None, None, ('dom', 'quad')), may hold values from -6 to 6
- star_matrices: float32 [3, 9, 9, 65536], P(None, None, None, ('dom', 'quad')), may hold values from -3 to 3
- face_normals: float32 [3, 4, 65536], P(None, None, ('dom', 'quad')), may hold values from -3 to 3
- wave_speed: float32 [65536], P(('dom', 'quad')), may hold values from 0.5 to 2
- stiffness: float32 [56, 3, 56], replicated, may hold values from -0.75 to 0.75
- face_projection: float32 [4, 21, 56], replicated, may hold values from -0.75 to 0.75
- face_lift: float32 [4, 56, 21], replicated, may hold values from -0.625 to 0.625
- friction_table: float32 [3, 8], replicated, may hold values from 0.2 to 1
- neighbour_index: int32 [4, 65536], P(None, ('dom', 'quad')), may hold values from 0 to 1535, as said below
- orientation: int32 [4, 65536], P(None, ('dom', 'quad')), may hold values from 0 to 5
- send_list: int32 [2, 65536], P(None, ('dom', 'quad')), may hold values from 0 to 1023
- fault_face: int32 [65536], P(('dom', 'quad')), may hold values from 0 to 1023, as said below
- fault_dest: int32 [65536], P(('dom', 'quad')), may hold values from -1 to 32767, as said below
- fault_region: int32 [16384], replicated, may hold values from 0 to 7
Outputs:
- updated_dofs: float32 [56, 9, 65536], P(None, None, ('dom', 'quad'))
The draws below stay inside these ranges and needn't reach their ends.
Inputs may be any that keep to these rules, and one draw needn't show every extreme that they name: `neighbour_index`: every halo column 1024 to 1535 is named by exactly one face of the partition; the other faces name its own columns. `fault_face`: the faces of one partition's fault slots are distinct, and none of them names a halo column in neighbour_index. `fault_dest`: owner o sits at dom index 8 (o // 4) and quad index o % 4. Every owner, pair and side appears in exactly one live slot over all partitions. At most 8 live slots of one partition name one owner, and for every owner some partition has exactly 8.
All inputs are finite; a program needn't handle non-finite values.
Results may differ from the reference program's by a relative error of at most 0.0003.
Values sent between devices are 32-bit elements; how exact they have to be, the bound alone decides.
A program may use at most 128 MiB of HBM per device.

```python
import math
import jax
import jax.numpy as jnp
import numpy as np
from jax import lax

BASIS = 56
FACE_BASIS = 21
QUANT = 9
ORDER = 6
NEWTON = 8
REGIONS = 8
CAP = 8
E_DEV = 256
HALO = 256
ELEMS = 65536
OWNERS = 32
FPO = 512
SENDS = 65536
PAIRS = 16384
N_DOM = 64
N_QUAD = 4


def fault_layout(key):
    devices_all = N_DOM * N_QUAD
    faces_dev = 4 * E_DEV
    slots_dev = CAP * OWNERS
    sides_owner = 2 * FPO
    base_key = jax.random.fold_in(key, 901)
    perm_keys = jax.random.split(jax.random.fold_in(base_key, 1), devices_all)
    orders = jax.vmap(lambda one_key: jax.random.permutation(one_key, faces_dev))(perm_keys)
    local_pick = jax.random.randint(jax.random.fold_in(base_key, 2), (devices_all, faces_dev), 0, faces_dev).astype(jnp.int32)

    def place_halo(order_row, pick_row):
        return pick_row.at[order_row[:2 * HALO]].set((faces_dev + jnp.arange(2 * HALO)).astype(jnp.int32))
    neighbours = jax.vmap(place_halo)(orders, local_pick)
    faults = orders[:, 2 * HALO:2 * HALO + slots_dev]
    half_pairs = devices_all // 2
    spread = jax.random.randint(jax.random.fold_in(base_key, 3), (half_pairs, OWNERS), 0, CAP // 2 + 1)
    forced = jax.random.randint(jax.random.fold_in(base_key, 4), (OWNERS,), 0, half_pairs)
    spread = jnp.where(jnp.arange(half_pairs)[:, None] == forced[None, :], CAP // 2, spread)
    flip_bits = jax.random.randint(jax.random.fold_in(base_key, 5), (half_pairs, OWNERS), 0, 2)
    first_count = CAP // 2 + spread * (1 - 2 * flip_bits)
    counts = jnp.stack([first_count, CAP - first_count], axis=1).reshape(devices_all, OWNERS)
    offsets = jnp.cumsum(counts, axis=0) - counts
    slot_keys = jax.random.split(jax.random.fold_in(base_key, 6), OWNERS)
    slot_orders = jax.vmap(lambda one_key: jax.random.permutation(one_key, sides_owner))(slot_keys)
    position = jnp.arange(slots_dev)
    owner_of = position // CAP
    within = position % CAP
    live_slot = within[None, :] < counts[:, owner_of]
    side_index = jnp.clip(offsets[:, owner_of] + within[None, :], 0, sides_owner - 1)
    side_slot = slot_orders[jnp.broadcast_to(owner_of[None, :], side_index.shape), side_index]
    destination = jnp.where(live_slot, owner_of[None, :] * sides_owner + side_slot, -1)
    list_keys = jax.random.split(jax.random.fold_in(base_key, 7), devices_all)
    shuffles = jax.vmap(lambda one_key: jax.random.permutation(one_key, slots_dev))(list_keys)
    destination = jnp.take_along_axis(destination, shuffles, axis=1)
    return (neighbours, faults, destination)


def draw_neighbour_index(key, part):
    neighbours, faults, destination = fault_layout(key)
    shaped = neighbours.reshape(N_DOM * N_QUAD, 4, E_DEV)
    return jnp.transpose(shaped, (1, 0, 2)).reshape(4, N_DOM * N_QUAD * E_DEV).astype(jnp.int32)


def draw_fault_face(key, part):
    neighbours, faults, destination = fault_layout(key)
    return faults.reshape(-1).astype(jnp.int32)


def draw_fault_dest(key, part):
    neighbours, faults, destination = fault_layout(key)
    return destination.reshape(-1).astype(jnp.int32)


def place_ends(values, key, smallest, largest):
    shape = values.shape
    index_at = [jax.random.randint(jax.random.fold_in(key, axis), (), 0, shape[axis]) for axis in range(len(shape))]
    values = values.at[tuple(index_at)].set(smallest)
    longest = shape.index(max(shape))
    index_at[longest] = (index_at[longest] + 1) % shape[longest]
    return values.at[tuple(index_at)].set(largest)


def levels(rng, shape, cuts, least, largest):
    level = 1.0
    for dim, shards_of in cuts:
        draws = jax.random.uniform(jax.random.fold_in(jax.random.fold_in(rng, 6), dim), (shards_of,), jnp.float32, least / len(cuts), largest / len(cuts))
        level = level * jnp.repeat(jnp.exp(draws), shape[dim] // shards_of).reshape((-1,) + (1,) * (len(shape) - 1 - dim))
    return level


def centred(stream_key, dims, scale, limit, shards=(), dtype=jnp.bfloat16):
    factor_of = levels(stream_key, dims, shards, -0.22, 0.18) if shards else 1.0
    entries = jax.random.normal(stream_key, dims, jnp.float32) * scale * factor_of
    return jnp.minimum(jnp.maximum(entries, -limit), limit).astype(dtype)


def setup_inputs(seed: int = 0) -> dict:
    key_of = jax.random.split(jax.random.key(seed), 15)
    return {
        "element_dofs": centred(key_of[0], (BASIS, QUANT, ELEMS), 1.0, 6.0, ((2, 256),), jnp.float32),
        "star_matrices": centred(key_of[1], (3, QUANT, QUANT, ELEMS), 0.5, 3.0, ((3, 256),), jnp.float32),
        "face_normals": centred(key_of[2], (3, 4, ELEMS), 0.6, 3.0, ((2, 256),), jnp.float32),
        "wave_speed": jnp.clip(jnp.exp(math.log(2.0) - 1.3862944 * jax.random.uniform(key_of[3], (ELEMS,), jnp.float32) ** levels(key_of[3], (ELEMS,), ((0, 256),), -0.2, 0.2)), 0.5, 2.0),
        "stiffness": centred(key_of[4], (BASIS, 3, BASIS), BASIS ** -0.5, 0.75, (), jnp.float32),
        "face_projection": centred(key_of[5], (4, FACE_BASIS, BASIS), BASIS ** -0.5, 0.75, (), jnp.float32),
        "face_lift": centred(key_of[6], (4, BASIS, FACE_BASIS), (4 * FACE_BASIS) ** -0.5, 0.625, (), jnp.float32),
        "friction_table": jnp.clip(jax.random.uniform(key_of[7], (3, REGIONS), jnp.float32, 0.2, 1.0), 0.2, 1.0),
        "neighbour_index": draw_neighbour_index(jax.random.fold_in(key_of[14], 71), 0),
        "orientation": place_ends(jax.random.randint(key_of[9], (4, ELEMS), 0, 6), jax.random.fold_in(key_of[9], 1), 0, 5).astype(jnp.int32),
        "send_list": place_ends(jax.random.randint(key_of[10], (2, SENDS), 0, 4 * E_DEV), jax.random.fold_in(key_of[10], 1), 0, (4 * E_DEV) - 1).astype(jnp.int32),
        "fault_face": draw_fault_face(jax.random.fold_in(key_of[14], 71), 0),
        "fault_dest": draw_fault_dest(jax.random.fold_in(key_of[14], 71), 0),
        "fault_region": place_ends(jax.random.randint(key_of[13], (PAIRS,), 0, REGIONS), jax.random.fold_in(key_of[13], 1), 0, REGIONS - 1).astype(jnp.int32),
    }


highest = lax.Precision.HIGHEST
relaxation = 0.4
eta_half = 0.5
time_step = 0.25
sigma_zero = 2.0
shear_scale = 3.0

def inverse_sinh(value):
    magnitude = jnp.abs(value)
    result = jnp.log(magnitude + jnp.sqrt(1.0 + magnitude * magnitude))
    return jnp.where(value < 0.0, -result, result)

def spatial(values, star_block, stiffness):
    basis_size, quant_size, elem_count = values.shape
    directions = []
    for direction in range(3):
        mixture = star_block[direction, :, 0, :][None] * values[:, 0, :][:, None, :]
        for column in range(1, quant_size):
            mixture = mixture + star_block[direction, :, column, :][None] * values[:, column, :][:, None, :]
        directions.append(mixture)
    stacked = jnp.stack(directions).reshape(3 * basis_size, quant_size * elem_count)
    product = jnp.dot(stiffness.reshape(basis_size, 3 * basis_size), stacked, precision=highest, preferred_element_type=jnp.float32)
    return product.reshape(basis_size, quant_size, elem_count)

def predict(values, star_block, stiffness):
    derivative = values
    integral = values
    for degree in range(1, ORDER):
        derivative = spatial(derivative, star_block, stiffness)
        integral = integral + derivative * (1.0 / math.factorial(degree + 1))
    return integral

def face_table(integral, face_projection):
    basis_size, quant_size, elem_count = integral.shape
    flattened = integral.reshape(basis_size, quant_size * elem_count)
    pieces = []
    for face_id in range(4):
        traced = jnp.dot(face_projection[face_id], flattened, precision=highest, preferred_element_type=jnp.float32)
        pieces.append(traced.reshape(-1, quant_size, elem_count))
    return jnp.concatenate(pieces, axis=2).reshape(-1, 4 * elem_count)

def reorient(raw_table, orientation_flat, quant_size):
    shaped = raw_table.reshape(-1, quant_size, raw_table.shape[1])
    face_size = shaped.shape[0]
    result = jnp.zeros_like(shaped)
    for variant in range(6):
        stride = 1 if variant < 3 else face_size - 1
        rows_order = np.array([(stride * position + face_size // 3 * (variant % 3)) % face_size for position in range(face_size)])
        result = jnp.where((orientation_flat == variant)[None, None, :], shaped[rows_order], result)
    return result.reshape(raw_table.shape)

def face_flux(own_table, outer_table, star_block, normals_block, speed_block):
    quant_size = star_block.shape[1]
    elem_count = star_block.shape[3]
    normals_flat = normals_block.reshape(3, 4 * elem_count)
    star_tiled = jnp.concatenate([star_block] * 4, axis=3)
    normal_matrix = normals_flat[0][None, None, :] * star_tiled[0]
    for direction in range(1, 3):
        normal_matrix = normal_matrix + normals_flat[direction][None, None, :] * star_tiled[direction]
    own_trace = own_table.reshape(-1, quant_size, 4 * elem_count)
    outer_trace = outer_table.reshape(-1, quant_size, 4 * elem_count)
    summed = own_trace + outer_trace
    central = normal_matrix[:, 0, :][None] * summed[:, 0, :][:, None, :]
    for column in range(1, quant_size):
        central = central + normal_matrix[:, column, :][None] * summed[:, column, :][:, None, :]
    speeds = jnp.concatenate([speed_block] * 4)
    return 0.5 * central + 0.5 * speeds[None, None, :] * (own_trace - outer_trace)

def apply_lift(dofs_block, volume, fluxes, face_lift):
    basis_size, quant_size, elem_count = dofs_block.shape
    lifted = jnp.zeros((basis_size, quant_size * elem_count), jnp.float32)
    for face_id in range(4):
        face_piece = fluxes[:, :, face_id * elem_count:(face_id + 1) * elem_count].reshape(-1, quant_size * elem_count)
        lifted = lifted + jnp.dot(face_lift[face_id], face_piece, precision=highest, preferred_element_type=jnp.float32)
    return dofs_block + time_step * (volume - lifted.reshape(basis_size, quant_size, elem_count))

def friction(side_rows, regions, friction_table):
    pair_count = side_rows.shape[0]
    shaped = side_rows.reshape(pair_count, 2, -1, QUANT)
    region_count = friction_table.shape[1]
    selector = (regions[:, None] == jnp.arange(region_count)[None, :]).astype(jnp.float32)
    params = jnp.dot(selector, friction_table.T, precision=highest, preferred_element_type=jnp.float32)
    rate_term = params[:, 0][:, None]
    state_term = params[:, 1][:, None]
    background = shear_scale * params[:, 2][:, None]
    first_side = shaped[:, 0]
    second_side = shaped[:, 1]
    pressure = 1.0 + jax.nn.softplus(sigma_zero - 0.5 * (first_side[..., 0] + second_side[..., 0]))
    locked = 0.5 * (first_side[..., 3] + second_side[..., 3]) + eta_half * (second_side[..., 7] - first_side[..., 7]) + background
    stiff_rate = 0.5 * jnp.exp(state_term / rate_term)
    slip_rate = jnp.zeros_like(locked)
    for passes in range(NEWTON):
        argument = stiff_rate * slip_rate
        mismatch = eta_half * slip_rate + pressure * rate_term * inverse_sinh(argument) - locked
        gradient = eta_half + pressure * rate_term * stiff_rate / jnp.sqrt(1.0 + argument * argument)
        slip_rate = slip_rate - relaxation * mismatch / gradient
    traction = locked - eta_half * slip_rate
    average = 0.5 * (first_side + second_side)
    average = average.at[..., 3].set(traction - background)
    first_state = average.at[..., 7].add(-0.5 * slip_rate)
    second_state = average.at[..., 7].add(0.5 * slip_rate)
    return jnp.stack([first_state, second_state], axis=1).reshape(pair_count * 2, -1)

def reference(element_dofs, star_matrices, face_normals, wave_speed, stiffness, face_projection, face_lift, friction_table, neighbour_index, orientation, send_list, fault_face, fault_dest, fault_region):
    device_count = N_DOM * N_QUAD
    dofs_dev = jnp.moveaxis(element_dofs.reshape(BASIS, QUANT, device_count, E_DEV), 2, 0)
    star_dev = jnp.moveaxis(star_matrices.reshape(3, QUANT, QUANT, device_count, E_DEV), 3, 0)
    normals_dev = jnp.moveaxis(face_normals.reshape(3, 4, device_count, E_DEV), 2, 0)
    speed_dev = wave_speed.reshape(device_count, E_DEV)
    neighbour_dev = jnp.moveaxis(neighbour_index.reshape(4, device_count, E_DEV), 1, 0).reshape(device_count, 4 * E_DEV)
    orient_dev = jnp.moveaxis(orientation.reshape(4, device_count, E_DEV), 1, 0).reshape(device_count, 4 * E_DEV)
    sends_dev = jnp.moveaxis(send_list.reshape(2, device_count, HALO), 1, 0)
    faces_dev = fault_face.reshape(device_count, -1)
    dests_dev = fault_dest.reshape(device_count, -1)

    def first_pass(inputs):
        dofs_block, star_block, send_block, face_block = inputs
        trace_table = face_table(predict(dofs_block, star_block, stiffness), face_projection)
        outgoing = jnp.stack([trace_table[:, send_block[0]], trace_table[:, send_block[1]]])
        return (outgoing, trace_table[:, face_block].T)
    outgoing, fault_rows = lax.map(first_pass, (dofs_dev, star_dev, sends_dev, faces_dev))
    by_position = outgoing.reshape(N_DOM, N_QUAD, 2, -1, HALO)
    from_lower = jnp.roll(by_position[:, :, 1], 1, axis=0).reshape(device_count, -1, HALO)
    from_upper = jnp.roll(by_position[:, :, 0], -1, axis=0).reshape(device_count, -1, HALO)
    side_total = 2 * FPO * OWNERS
    live_slot = fault_dest >= 0
    rows_flat = fault_rows.reshape(-1, fault_rows.shape[2])
    side_rows = jnp.zeros((side_total, rows_flat.shape[1]), jnp.float32)
    side_rows = side_rows.at[jnp.where(live_slot, fault_dest, side_total)].set(rows_flat, mode='drop')
    imposed = friction(side_rows.reshape(FPO * OWNERS, 2, -1), fault_region, friction_table)
    answers = imposed[jnp.clip(fault_dest, 0, side_total - 1)] * live_slot[:, None].astype(jnp.float32)
    answers_dev = answers.reshape(device_count, -1, answers.shape[1])

    def second_pass(inputs):
        dofs_block, star_block, normals_block, speed_block, neighbour_block, orient_block, face_block, dest_block, answer_block, lower_block, upper_block = inputs
        integral = predict(dofs_block, star_block, stiffness)
        trace_table = face_table(integral, face_projection)
        extended = jnp.concatenate([trace_table, lower_block, upper_block], axis=1)
        outer_table = reorient(extended[:, neighbour_block], orient_block, QUANT)
        live_block = dest_block >= 0
        faces_total = trace_table.shape[1]
        virtual = 2.0 * answer_block - trace_table[:, face_block].T
        outer_table = outer_table.at[:, jnp.where(live_block, face_block, faces_total)].set(virtual.T, mode='drop')
        fluxes = face_flux(trace_table, outer_table, star_block, normals_block, speed_block)
        volume = spatial(integral, star_block, stiffness)
        return apply_lift(dofs_block, volume, fluxes, face_lift)
    updated = lax.map(second_pass, (dofs_dev, star_dev, normals_dev, speed_dev, neighbour_dev, orient_dev, faces_dev, dests_dev, answers_dev, from_lower, from_upper))
    return jnp.moveaxis(updated, 0, 2).reshape(BASIS, QUANT, -1)
```

```python
import functools
import math

import jax
import jax.numpy as jnp
from jax import lax
from jax.experimental import pallas as pl
from jax.experimental.pallas import tpu as pltpu
from jax.sharding import PartitionSpec as P

ORDER = 6
NEWTON = 8
BASIS = 56
QUANT = 9
ELEM = 256
COLS = 4 * ELEM
ROWS = 24
COMPS = 224
LANES = 256
CODE, PARTNER = 216, 217
f32, bf16 = jnp.float32, jnp.bfloat16
MESH = pl.DeviceIdType.MESH
VMEM_LIMIT = 56 * 1024 * 1024


def iota(shape, dim):
    return lax.broadcasted_iota(jnp.int32, shape, dim)


def one_hot(mask):
    return jnp.where(mask, 1.0, 0.0).astype(bf16)


def split2(x):
    high = x.astype(bf16).astype(f32)
    return jnp.concatenate([high, x - high], axis=0).astype(bf16)


def split3(x):
    high = x.astype(bf16).astype(f32)
    return jnp.concatenate([high, x - high, high], axis=0).astype(bf16)


def dot(a, b):
    return jnp.dot(a, b, preferred_element_type=f32)


def halves(x):
    n = x.shape[0] // 2
    return x[:n] + x[n:]


def to_col(row):
    n = row.shape[1]
    eye = iota((n, n), 0) == iota((n, n), 1)
    return jnp.sum(jnp.where(eye, row, 0.0), axis=1, keepdims=True)


def to_row(col):
    n = col.shape[0]
    eye = iota((n, n), 0) == iota((n, n), 1)
    return jnp.sum(jnp.where(eye, col, 0.0), axis=0, keepdims=True)


def slot_rows(dest, face):
    n = dest.shape[1]
    live = dest >= 0
    owner = jnp.where(live, dest // 1024, 64).astype(f32)
    code = jnp.where(live, dest % 1024, -1).astype(f32)
    owner_col = to_col(owner)
    earlier = (owner_col == owner) & (iota((n, n), 0) < iota((n, n), 1))
    rank = jnp.sum(jnp.where(earlier, 1.0, 0.0), axis=0, keepdims=True)
    place = jnp.where(live, owner * 8.0 + rank, -1.0)
    put = to_col(place) == iota((n, n), 1).astype(f32)
    face_at = jnp.sum(jnp.where(put, to_col(face.astype(f32) + 1.0), 0.0), axis=0, keepdims=True)
    code_at = jnp.sum(jnp.where(put, to_col(code + 1.0), 0.0), axis=0, keepdims=True)
    return face_at - 1.0, code_at - 1.0


def spatial(load, star_ref, kmat_ref, mixed, store):
    for r in range(QUANT):
        mixed[r] = dot(kmat_ref[...], split3(load(r)))
    for tile in range(ELEM // 128):
        lanes = pl.ds(tile * 128, 128)
        for first in range(0, QUANT, 3):
            total = [None] * 3
            for d in range(3):
                for r in range(QUANT):
                    value = mixed[r, pl.ds(d * BASIS, BASIS), lanes]
                    for i in range(3):
                        term = star_ref[d, first + i, pl.ds(r, 1), lanes] * value
                        total[i] = term if total[i] is None else total[i] + term
            for i in range(3):
                store(first + i, lanes, total[i])


def predict_body(
    x_ref, star_ref, kmat_ref, proj_ref, send_ref, face_ref, dest_ref,
    integral_ref, trace_ref, halo_ref, slots_ref, rows_ref, mixed, deriv,
):
    for r in range(QUANT):
        value = x_ref[r]
        deriv[r] = value
        integral_ref[r] = value

    def degree(k, scale):
        scale = scale / (k + 1).astype(f32)

        def store(q, lanes, value):
            deriv[q, :, lanes] = value
            integral_ref[q, :, lanes] += value * scale

        spatial(lambda r: deriv[r], star_ref, kmat_ref, mixed, store)
        return scale

    lax.fori_loop(1, ORDER, degree, jnp.float32(1.0))

    for r in range(QUANT):
        traced = dot(proj_ref[...], split3(integral_ref[r]))
        for f in range(4):
            trace_ref[pl.ds(r * ROWS, ROWS), pl.ds(f * ELEM, ELEM)] = traced[f * ROWS : (f + 1) * ROWS]
    trace_ref[pl.ds(QUANT * ROWS, COMPS - QUANT * ROWS), :] = jnp.zeros((COMPS - QUANT * ROWS, COLS), f32)
    table = split2(trace_ref[...])
    face_at, code_at = slot_rows(dest_ref[...], face_ref[...])
    column = iota((COLS, 256), 0)
    slots = halves(dot(table, one_hot(column == face_at.astype(jnp.int32))))
    slots_ref[...] = slots
    rows = jnp.concatenate([slots, jnp.zeros((LANES - COMPS, 256), f32)], axis=0)
    whole = code_at.astype(jnp.int32)
    partner = jnp.where(whole >= 0, whole + 1 - 2 * (whole % 2), -5).astype(f32)
    row_of = iota((LANES, 256), 0)
    rows = jnp.where(row_of == CODE, code_at, jnp.where(row_of == PARTNER, partner, rows))
    rows_ref[...] = rows.T
    for side in range(2):
        halo_ref[side] = halves(dot(table, one_hot(column == send_ref[pl.ds(side, 1), :])))


def vmem(n):
    return [pl.BlockSpec(memory_space=pltpu.VMEM)] * n


def predict(x, star, kmat, proj, send, face, dest):
    shape = jax.ShapeDtypeStruct
    return pl.pallas_call(
        predict_body,
        out_shape=(
            shape((QUANT, BASIS, ELEM), f32),
            shape((COMPS, COLS), f32),
            shape((2, COMPS, 256), f32),
            shape((COMPS, 256), f32),
            shape((256, LANES), f32),
        ),
        in_specs=vmem(7),
        out_specs=tuple(vmem(5)),
        scratch_shapes=[
            pltpu.VMEM((QUANT, 3 * BASIS, ELEM), f32),
            pltpu.VMEM((QUANT, BASIS, ELEM), f32),
        ],
        compiler_params=pltpu.CompilerParams(vmem_limit_bytes=VMEM_LIMIT),
    )(x, star, kmat, proj, send, face, dest)


def exchange_body(
    rows_ref, halo_ref, back_ref, outer_halo_ref,
    held, replies, halo_in, back,
    halo_send, halo_recv, out_send, out_recv, ring_send, ring_recv, side_send, side_recv, back_send, back_recv, local_sem,
):
    dom, quad = lax.axis_index("dom"), lax.axis_index("quad")
    doms = lax.axis_size("dom")
    block, member = dom // 8, dom % 8
    y, core = member // 2, member % 2
    base = block * 8
    own = block * 4 + quad
    up, down, far = (y + 1) % 4, (y + 3) % 4, (y + 2) % 4
    upper, lower = lax.rem(dom + 1, doms), lax.rem(dom + doms - 1, doms)

    def slot(yy, cc):
        return yy * 2 + cc

    def peer(o):
        return ((o // 4) * 8 + member, o % 4)

    barrier = pltpu.get_barrier_semaphore()

    def greet(i, carry):
        o = lax.rem(own + i, 32)
        pl.semaphore_signal(barrier, inc=1, device_id=peer(o), device_id_type=MESH)
        return carry

    lax.fori_loop(1, 32, greet, 0)
    neighbours = [(base + slot(up, core), quad), (base + slot(down, core), quad), (base + slot(y, 1 - core), quad), (upper, quad), (lower, quad)]
    for device in neighbours:
        pl.semaphore_signal(barrier, inc=1, device_id=device, device_id_type=MESH)
    pl.semaphore_wait(barrier, 31 + 5)

    def remote(src, dst, send_sem, recv_sem, device):
        return pltpu.make_async_remote_copy(
            src_ref=src, dst_ref=dst, send_sem=send_sem, recv_sem=recv_sem, device_id=device, device_id_type=MESH
        )

    def push(i, carry):
        o = lax.rem(own + i, 32)
        remote(rows_ref.at[o], held.at[member, own], out_send, out_recv, peer(o)).start()
        return carry

    lax.fori_loop(1, 32, push, 0)
    mine = pltpu.make_async_copy(rows_ref.at[own], held.at[member, own], local_sem)
    mine.start()
    low = remote(halo_ref.at[0], halo_in.at[1], halo_send.at[0], halo_recv.at[1], (lower, quad))
    high = remote(halo_ref.at[1], halo_in.at[0], halo_send.at[1], halo_recv.at[0], (upper, quad))
    low.start()
    high.start()
    mine.wait()
    all_but_one = remote(rows_ref.at[pl.ds(0, 31)], held.at[member, pl.ds(0, 31)], out_send, out_recv, peer(own))
    all_but_one.wait_send()
    all_but_one.wait_recv()

    mem_down, mem_up, mem_far = slot(down, core), slot(up, core), slot(far, core)
    to_up, to_down, to_side = neighbours[0], neighbours[1], neighbours[2]
    first, second = pl.ds(0, 16), pl.ds(16, 16)
    ring = [
        remote(held.at[member], held.at[member], ring_send.at[0], ring_recv.at[0], to_up),
        remote(held.at[member], held.at[member], ring_send.at[1], ring_recv.at[1], to_down),
    ]
    side = [remote(held.at[member], held.at[member], side_send.at[0], side_recv.at[0], to_side)]
    ring[0].start()
    ring[1].start()
    side[0].start()

    want = held[member].reshape(256, LANES)[:, PARTNER : PARTNER + 1]

    def matched(m):
        rows = held[m].reshape(256, LANES)
        code = to_row(rows[:, CODE : CODE + 1])
        pick = one_hot(want == code)
        high = rows.astype(bf16)
        low = (rows - high.astype(f32)).astype(bf16)
        return dot(pick, high) + dot(pick, low)

    total = matched(member)
    arrived = remote(held.at[mem_down], held.at[mem_down], ring_send.at[0], ring_recv.at[0], to_up)
    arrived.wait_recv()
    ring.append(remote(held.at[mem_down, first], held.at[mem_down, first], ring_send.at[2], ring_recv.at[2], to_up))
    ring[2].start()
    side.append(remote(held.at[mem_down], held.at[mem_down], side_send.at[1], side_recv.at[1], to_side))
    side[1].start()
    arrived = remote(held.at[mem_up], held.at[mem_up], ring_send.at[1], ring_recv.at[1], to_down)
    arrived.wait_recv()
    ring.append(remote(held.at[mem_up, second], held.at[mem_up, second], ring_send.at[3], ring_recv.at[3], to_down))
    ring[3].start()
    side.append(remote(held.at[mem_up], held.at[mem_up], side_send.at[2], side_recv.at[2], to_side))
    side[2].start()
    total += matched(mem_down)
    total += matched(mem_up)
    side_mem = [slot(yy, 1 - core) for yy in (y, down, up, far)]
    for i in range(3):
        remote(held.at[side_mem[i]], held.at[side_mem[i]], side_send.at[i], side_recv.at[i], to_side).wait_recv()
        total += matched(side_mem[i])
    for i, part in ((2, first), (3, second)):
        remote(held.at[mem_far, part], held.at[mem_far, part], ring_send.at[i], ring_recv.at[i], to_up).wait_recv()
        side.append(remote(held.at[mem_far, part], held.at[mem_far, part], side_send.at[i + 1], side_recv.at[i + 1], to_side))
        side[i + 1].start()
    total += matched(mem_far)
    for i, part in ((3, first), (4, second)):
        remote(held.at[side_mem[3], part], held.at[side_mem[3], part], side_send.at[i], side_recv.at[i], to_side).wait_recv()
    total += matched(side_mem[3])
    replies[...] = total.reshape(32, 8, LANES)

    def reply(i, carry):
        o = lax.rem(own + i, 32)
        remote(replies.at[o], back.at[own], back_send, back_recv, peer(o)).start()
        return carry

    lax.fori_loop(1, 32, reply, 0)
    mine = pltpu.make_async_copy(replies.at[own], back.at[own], local_sem)
    mine.start()
    for copy in ring + side:
        copy.wait_send()
    low.wait_send()
    high.wait_send()
    remote(halo_ref.at[1], halo_in.at[0], halo_send.at[1], halo_recv.at[0], (upper, quad)).wait_recv()
    remote(halo_ref.at[0], halo_in.at[1], halo_send.at[0], halo_recv.at[1], (lower, quad)).wait_recv()
    outer_halo_ref[...] = halo_in[...]
    mine.wait()
    all_but_one = remote(replies.at[pl.ds(0, 31)], back.at[pl.ds(0, 31)], back_send, back_recv, peer(own))
    all_but_one.wait_send()
    all_but_one.wait_recv()
    back_ref[...] = back[...]


def exchange(rows, halo):
    dma = pltpu.SemaphoreType.DMA
    shape = jax.ShapeDtypeStruct
    return pl.pallas_call(
        exchange_body,
        out_shape=(shape((32, 8, LANES), f32), shape((2, COMPS, 256), f32)),
        in_specs=vmem(2),
        out_specs=tuple(vmem(2)),
        scratch_shapes=[
            pltpu.VMEM((8, 32, 8, LANES), f32),
            pltpu.VMEM((32, 8, LANES), f32),
            pltpu.VMEM((2, COMPS, 256), f32),
            pltpu.VMEM((32, 8, LANES), f32),
            dma((2,)), dma((2,)), dma, dma, dma((4,)), dma((4,)), dma((5,)), dma((5,)), dma, dma, dma,
        ],
        compiler_params=pltpu.CompilerParams(collective_id=0, has_side_effects=True, vmem_limit_bytes=VMEM_LIMIT),
    )(rows.reshape(32, 8, LANES), halo)


def inverse_sinh(value):
    magnitude = jnp.abs(value)
    result = jnp.log(magnitude + jnp.sqrt(1.0 + magnitude * magnitude))
    return jnp.where(value < 0.0, -result, result)


def friction_params(code_at, region_ref, table_ref):
    code_col = to_col(code_at).astype(jnp.int32)
    pair = code_col // 2
    n_pairs = region_ref.shape[1]
    regions = jnp.broadcast_to(region_ref[...].astype(f32)[:, None, :], (32, 8, n_pairs)).reshape(256, n_pairs)
    hit = (pair == iota((256, n_pairs), 1)) & (code_col >= 0)
    region = to_row(jnp.sum(jnp.where(hit, regions, 0.0), axis=1, keepdims=True))
    params = []
    for row in range(3):
        value = jnp.full((1, 256), table_ref[row, 0], f32)
        for j in range(1, 8):
            value = jnp.where(region == float(j), table_ref[row, j], value)
        params.append(value)
    return params


def friction(own, other, code_at, params):
    rate_term, state_term, shear = params
    background = 3.0 * shear

    def comp(x, r):
        return x[r * ROWS : (r + 1) * ROWS]

    second = (code_at.astype(jnp.int32) % 2) == 1
    sign = jnp.where(second, -1.0, 1.0)
    pressure = 1.0 + jax.nn.softplus(2.0 - 0.5 * (comp(own, 0) + comp(other, 0)))
    locked = (
        0.5 * (comp(own, 3) + comp(other, 3)) + 0.5 * sign * (comp(other, 7) - comp(own, 7)) + background
    )
    stiff_rate = 0.5 * jnp.exp(state_term / rate_term)
    slip = jnp.zeros_like(locked)
    for _ in range(NEWTON):
        argument = stiff_rate * slip
        mismatch = 0.5 * slip + pressure * rate_term * inverse_sinh(argument) - locked
        gradient = 0.5 + pressure * rate_term * stiff_rate / jnp.sqrt(1.0 + argument * argument)
        slip = slip - 0.4 * mismatch / gradient
    third = 2.0 * (locked - 0.5 * slip - background) - comp(own, 3)
    seventh = comp(other, 7) - sign * slip
    return jnp.concatenate(
        [other[: 3 * ROWS], third, other[4 * ROWS : 7 * ROWS], seventh, other[8 * ROWS : QUANT * ROWS]], axis=0
    )


def flip(x):
    index = 7 - iota((8, 128), 0)
    parts = [
        jnp.take_along_axis(x[:, c : c + 128], index, axis=0, mode="promise_in_bounds") for c in range(0, x.shape[1], 128)
    ]
    return jnp.concatenate(parts, axis=1)


def finish_body(
    x_ref, star_ref, kmat_ref, lift_ref, integral_ref, trace_ref, halo_ref, slots_ref, back_ref,
    index_ref, orient_ref, normals_ref, speed_ref, face_ref, dest_ref, region_ref, table_ref,
    out_ref, mixed, volume, outer, matrix, fluxes,
):
    face_at, code_at = slot_rows(dest_ref[...], face_ref[...])
    other = back_ref[...].reshape(256, LANES).T
    params = friction_params(code_at, region_ref, table_ref)
    imposed = split2(
        jnp.concatenate(
            [friction(slots_ref[...], other, code_at, params), jnp.zeros((COMPS - QUANT * ROWS, 256), f32)], axis=0
        )
    )
    face_col = to_col(face_at).astype(jnp.int32)
    table = split2(trace_ref[...])
    halo = [split2(halo_ref[0]), split2(halo_ref[1])]
    first = iota((8, ELEM), 0) == 0
    for f in range(4):
        cols = pl.ds(f * ELEM, ELEM)
        index = index_ref[pl.ds(f, 1), :]
        raw = dot(table, one_hot(iota((COLS, ELEM), 0) == index))
        for side in range(2):
            raw += dot(halo[side], one_hot(iota((256, ELEM), 0) + (COLS + 256 * side) == index))
        raw = halves(raw)
        put = face_col == iota((256, ELEM), 1) + f * ELEM
        fault = halves(dot(imposed, one_hot(put)))
        is_fault = jnp.sum(jnp.where(put, 1.0, 0.0), axis=0, keepdims=True) > 0.5
        orient = orient_ref[pl.ds(f, 1), :]
        turn = orient % 3
        back = orient >= 3
        for r in range(QUANT):
            group = [raw[r * ROWS + 8 * g : r * ROWS + 8 * g + 8] for g in range(3)]
            moved = [
                jnp.where(turn == 0, group[g], jnp.where(turn == 1, group[(g + 1) % 3], group[(g + 2) % 3]))
                for g in range(3)
            ]
            for g in range(3):
                reverse = jnp.where(first, moved[(3 - g) % 3], flip(moved[(5 - g) % 3]))
                value = jnp.where(back, reverse, moved[g])
                at = r * ROWS + 8 * g
                outer[pl.ds(at, 8), cols] = jnp.where(is_fault, fault[at : at + 8], value)

    for f in range(4):
        for r in range(QUANT):
            total = normals_ref[0, pl.ds(f, 1), :] * star_ref[0, r]
            for d in range(1, 3):
                total += normals_ref[d, pl.ds(f, 1), :] * star_ref[d, r]
            matrix[f, r] = 0.5 * total

    for f in range(4):
        for tile in range(ELEM // 128):
            lanes = pl.ds(tile * 128, 128)
            cols = pl.ds(f * ELEM + tile * 128, 128)
            speed = 0.5 * speed_ref[:, lanes]
            for chunk in range(3):
                at = [pl.ds(r * ROWS + 8 * chunk, 8) for r in range(QUANT)]
                summed = [trace_ref[at[t], cols] + outer[at[t], cols] for t in range(QUANT)]
                for r in range(QUANT):
                    total = speed * (trace_ref[at[r], cols] - outer[at[r], cols])
                    for t in range(QUANT):
                        total += matrix[f, r, pl.ds(t, 1), lanes] * summed[t]
                    fluxes[r, pl.ds(f * ROWS + 8 * chunk, 8), lanes] = total

    def store(q, lanes, value):
        volume[q, :, lanes] = value

    spatial(lambda r: integral_ref[r], star_ref, kmat_ref, mixed, store)
    for r in range(QUANT):
        lifted = dot(lift_ref[...], split3(fluxes[r]))
        out_ref[r] = x_ref[r] + 0.25 * (volume[r] - lifted)


def finish(x, star, kmat, lift, integral, trace, halo, slots, back, index, orient, normals, speed, face, dest, region, table):
    return pl.pallas_call(
        finish_body,
        out_shape=jax.ShapeDtypeStruct((QUANT, BASIS, ELEM), f32),
        in_specs=vmem(16) + [pl.BlockSpec(memory_space=pltpu.SMEM)],
        out_specs=vmem(1)[0],
        scratch_shapes=[
            pltpu.VMEM((QUANT, 3 * BASIS, ELEM), f32),
            pltpu.VMEM((QUANT, BASIS, ELEM), f32),
            pltpu.VMEM((COMPS, COLS), f32),
            pltpu.VMEM((4, QUANT, QUANT, ELEM), f32),
            pltpu.VMEM((QUANT, 4 * ROWS, ELEM), f32),
        ],
        compiler_params=pltpu.CompilerParams(vmem_limit_bytes=VMEM_LIMIT),
    )(x, star, kmat, lift, integral, trace, halo, slots, back, index, orient, normals, speed, face, dest, region, table)


def parts(weights):
    high = lax.reduce_precision(weights, 8, 7)
    return jnp.concatenate([high, high, weights - high], axis=-1).astype(bf16)


def weights_of(stiffness, face_projection, face_lift):
    kmat = parts(jnp.transpose(stiffness, (1, 0, 2)).reshape(3 * BASIS, BASIS))
    pad = ((0, 0), (0, 0), (0, 1), (0, 0))
    proj = parts(jnp.pad(face_projection.reshape(4, 3, 7, BASIS), pad).reshape(4 * ROWS, BASIS))
    lift = jnp.pad(jnp.transpose(face_lift, (1, 0, 2)).reshape(BASIS, 4, 3, 7), ((0, 0), (0, 0), (0, 0), (0, 1)))
    return kmat, proj, parts(lift.reshape(BASIS, 4 * ROWS))


def local(
    element_dofs, star_matrices, face_normals, wave_speed, stiffness, face_projection, face_lift, friction_table,
    neighbour_index, orientation, send_list, fault_face, fault_dest, fault_region,
):
    kmat, proj, lift = weights_of(stiffness, face_projection, face_lift)
    x = jnp.transpose(element_dofs, (1, 0, 2))
    face, dest = fault_face.reshape(1, -1), fault_dest.reshape(1, -1)
    integral, trace, halo, slots, rows = predict(x, star_matrices, kmat, proj, send_list, face, dest)
    back, outer_halo = exchange(rows, halo)
    out = finish(
        x, star_matrices, kmat, lift, integral, trace, outer_halo, slots, back, neighbour_index, orientation,
        face_normals, wave_speed.reshape(1, -1), face, dest, fault_region.reshape(32, -1), friction_table,
    )
    return jnp.transpose(out, (1, 0, 2))


def solution(mesh):
    return jax.shard_map(
        local,
        mesh=mesh,
        in_specs=(
            P(None, None, ("dom", "quad")),
            P(None, None, None, ("dom", "quad")),
            P(None, None, ("dom", "quad")),
            P(("dom", "quad")),
            P(),
            P(),
            P(),
            P(),
            P(None, ("dom", "quad")),
            P(None, ("dom", "quad")),
            P(None, ("dom", "quad")),
            P(("dom", "quad")),
            P(("dom", "quad")),
            P(),
        ),
        out_specs=P(None, None, ("dom", "quad")),
        check_vma=False,
    )
```

```python
import functools
import math

import jax
import jax.numpy as jnp
from jax import lax
from jax.experimental import pallas as pl
from jax.experimental.pallas import tpu as pltpu
from jax.sharding import PartitionSpec as P

ORDER = 6
NEWTON = 8
BASIS = 56
QUANT = 9
ELEM = 256
COLS = 4 * ELEM
ROWS = 24
COMPS = 224
WIRE = 192
CODE, PARTNER = 189, 190
PIECES = 4
f32, bf16 = jnp.float32, jnp.bfloat16
MESH = pl.DeviceIdType.MESH
VMEM_LIMIT = 56 * 1024 * 1024


def iota(shape, dim):
    return lax.broadcasted_iota(jnp.int32, shape, dim)


def one_hot(mask):
    return jnp.where(mask, 1.0, 0.0).astype(bf16)


def split2(x):
    high = x.astype(bf16).astype(f32)
    return jnp.concatenate([high, x - high], axis=0).astype(bf16)


def split3(x):
    high = x.astype(bf16).astype(f32)
    return jnp.concatenate([high, x - high, high], axis=0).astype(bf16)


def dot(a, b):
    return jnp.dot(a, b, preferred_element_type=f32)


def halves(x):
    n = x.shape[0] // 2
    return x[:n] + x[n:]


def to_col(row):
    n = row.shape[1]
    eye = iota((n, n), 0) == iota((n, n), 1)
    return jnp.sum(jnp.where(eye, row, 0.0), axis=1, keepdims=True)


def to_row(col):
    n = col.shape[0]
    eye = iota((n, n), 0) == iota((n, n), 1)
    return jnp.sum(jnp.where(eye, col, 0.0), axis=0, keepdims=True)


def slot_rows(dest, face):
    n = dest.shape[1]
    live = dest >= 0
    owner = jnp.where(live, dest // 1024, 64).astype(f32)
    code = jnp.where(live, dest % 1024, -1).astype(f32)
    owner_col = to_col(owner)
    earlier = (owner_col == owner) & (iota((n, n), 0) < iota((n, n), 1))
    rank = jnp.sum(jnp.where(earlier, 1.0, 0.0), axis=0, keepdims=True)
    place = jnp.where(live, owner * 8.0 + rank, -1.0)
    put = to_col(place) == iota((n, n), 1).astype(f32)
    face_at = jnp.sum(jnp.where(put, to_col(face.astype(f32) + 1.0), 0.0), axis=0, keepdims=True)
    code_at = jnp.sum(jnp.where(put, to_col(code + 1.0), 0.0), axis=0, keepdims=True)
    return face_at - 1.0, code_at - 1.0


def packed(first, second):
    swapped = pltpu.roll(pltpu.roll(second, 64, 1), 252, 0)
    pairs = jnp.where(iota((256, 128), 1) < 64, second, swapped)
    return first.reshape(32, 8, 128), pairs.reshape(32, 8, 128)[:, :4, :]


def put_packed(ref, first, second):
    ref[:, pl.ds(0, 8), :], ref[:, pl.ds(8, 4), :] = packed(first, second)


def unpacked(ref, *at):
    first = ref[(*at, slice(None), pl.ds(0, 8), slice(None))].reshape(256, 128)
    pairs = ref[(*at, slice(None), pl.ds(8, 4), slice(None))]
    pairs = jnp.concatenate([pairs, pairs], axis=1).reshape(256, 128)
    second = jnp.where(iota((256, 128), 0) % 8 < 4, pairs, pltpu.roll(pairs, 64, 1))
    return first, second


def narrow():
    value, row = iota((WIRE, 2 * COMPS), 0), iota((WIRE, 2 * COMPS), 1)
    row = jnp.where(row >= COMPS, row - COMPS, row)
    return one_hot((row == value + ((value * 9363) >> 16)) & (value < CODE))


def widen():
    row, value = iota((COMPS, 2 * WIRE), 0), iota((COMPS, 2 * WIRE), 1)
    value = jnp.where(value >= WIRE, value - WIRE, value)
    return one_hot((row == value + ((value * 9363) >> 16)) & (value < CODE))


def weight_parts(weights):
    high = weights.astype(bf16).astype(f32)
    return jnp.concatenate([high, high, weights - high], axis=1).astype(bf16)


def spatial_products(load, kmat_ref, mixed):
    for r in range(QUANT):
        mixed[r] = dot(kmat_ref[...], split3(load(r)))


def spatial_mix(tile, firsts, star_ref, mixed, store):
    lanes = pl.ds(tile * 128, 128)
    for first in firsts:
        total = [None] * 3
        for d in range(3):
            for r in range(QUANT):
                value = mixed[r, pl.ds(d * BASIS, BASIS), lanes]
                for i in range(3):
                    term = star_ref[d, first + i, pl.ds(r, 1), lanes] * value
                    total[i] = term if total[i] is None else total[i] + term
        for i in range(3):
            store(first + i, lanes, total[i])


def inverse_sinh(value):
    magnitude = jnp.abs(value)
    result = jnp.log(magnitude + jnp.sqrt(1.0 + magnitude * magnitude))
    return jnp.where(value < 0.0, -result, result)


def friction_params(code_at, region_ref, table_ref):
    code_col = to_col(code_at).astype(jnp.int32)
    pairs = region_ref.shape[1] // 32
    regions = jnp.concatenate(
        [jnp.broadcast_to(region_ref[:, pl.ds(o * pairs, pairs)], (8, pairs)) for o in range(32)], axis=0
    ).astype(f32)
    hit = (code_col // 2 == iota((256, pairs), 1)) & (code_col >= 0)
    region = to_row(jnp.sum(jnp.where(hit, regions, 0.0), axis=1, keepdims=True))
    params = []
    for row in range(3):
        value = jnp.full((1, 256), table_ref[row, 0], f32)
        for j in range(1, 8):
            value = jnp.where(region == float(j), table_ref[row, j], value)
        params.append(value)
    return params


def friction(own, other, code_at, params):
    rate_term, state_term, shear = params
    background = 3.0 * shear

    def comp(x, r):
        return x[r * ROWS : (r + 1) * ROWS]

    second = (code_at.astype(jnp.int32) % 2) == 1
    sign = jnp.where(second, -1.0, 1.0)
    pressure = 1.0 + jax.nn.softplus(2.0 - 0.5 * (comp(own, 0) + comp(other, 0)))
    locked = (
        0.5 * (comp(own, 3) + comp(other, 3)) + 0.5 * sign * (comp(other, 7) - comp(own, 7)) + background
    )
    stiff_rate = 0.5 * jnp.exp(state_term / rate_term)
    slip = jnp.zeros_like(locked)
    for _ in range(NEWTON):
        argument = stiff_rate * slip
        mismatch = 0.5 * slip + pressure * rate_term * inverse_sinh(argument) - locked
        gradient = 0.5 + pressure * rate_term * stiff_rate / jnp.sqrt(1.0 + argument * argument)
        slip = slip - 0.4 * mismatch / gradient
    third = 2.0 * (locked - 0.5 * slip - background) - comp(own, 3)
    seventh = comp(other, 7) - sign * slip
    return jnp.concatenate(
        [other[: 3 * ROWS], third, other[4 * ROWS : 7 * ROWS], seventh, other[8 * ROWS : QUANT * ROWS]], axis=0
    )


def flip(x):
    index = 7 - iota((8, 128), 0)
    parts = [
        jnp.take_along_axis(x[:, c : c + 128], index, axis=0, mode="promise_in_bounds") for c in range(0, x.shape[1], 128)
    ]
    return jnp.concatenate(parts, axis=1)


def step_body(
    x_ref, star_in, stiff_ref, proj_in, lift_in, normals_ref, speed_ref, index_ref, orient_ref, send_ref, face_ref,
    dest_ref, region_ref, table_ref,
    change_ref,
    star, kmat, proj, lift, mixed, deriv, integral, volume, trace, table, slots, raw, matrix, fluxes, points, params,
    rows, held, replies, back, halo_out, halo_in,
    halo_send, halo_recv, out_send, out_recv, ring_send, ring_recv, side_send, side_recv, back_send, back_recv, local_sem,
):
    dom, quad = lax.axis_index("dom"), lax.axis_index("quad")
    doms = lax.axis_size("dom")
    block, member = dom // 8, dom % 8
    y, core = member // 2, member % 2
    own = block * 4 + quad

    def slot(yy, cc):
        return yy * 2 + cc

    def peer(o):
        return ((o // 4) * 8 + member, o % 4)

    up, down, far = (y + 1) % 4, (y + 3) % 4, (y + 2) % 4
    mem_up, mem_down, mem_far = slot(up, core), slot(down, core), slot(far, core)
    to_up, to_down = (block * 8 + mem_up, quad), (block * 8 + mem_down, quad)
    to_side = (block * 8 + slot(y, 1 - core), quad)
    upper, lower = (lax.rem(dom + 1, doms), quad), (lax.rem(dom + doms - 1, doms), quad)

    barrier = pltpu.get_barrier_semaphore()

    def greet(i, carry):
        pl.semaphore_signal(barrier, inc=1, device_id=peer(lax.rem(own + i, 32)), device_id_type=MESH)
        return carry

    lax.fori_loop(1, 32, greet, 0)
    for device in (to_up, to_down, to_side, upper, lower):
        pl.semaphore_signal(barrier, inc=1, device_id=device, device_id_type=MESH)

    for q in range(QUANT):
        for r in range(QUANT):
            star[:, q, r, :] = star_in[q, r]
    kmat[...] = weight_parts(stiff_ref[...])
    for source, padded in ((proj_in, points.at[0]), (lift_in, points.at[1])):
        padded[...] = jnp.zeros_like(padded)
        for p in range(21):
            padded[:, p // 7 * 8 + p % 7, :] = source[p]
    proj[...] = weight_parts(points[0].reshape(4 * ROWS, BASIS))
    lift[...] = weight_parts(
        jnp.concatenate(
            [
                jnp.concatenate([points[1].reshape(4 * ROWS, BASIS), jnp.zeros((4 * ROWS, 128 - BASIS), f32)], axis=1),
                jnp.zeros((128 - 4 * ROWS, 128), f32),
            ],
            axis=0,
        ).T[:BASIS, : 4 * ROWS]
    )
    face_at, code_at = slot_rows(dest_ref[...], face_ref[...])

    for r in range(QUANT):
        value = x_ref[r]
        deriv[r] = value
        integral[r] = value

    def degree(k, scale):
        scale = scale / (k + 1).astype(f32)

        def store(q, lanes, value):
            deriv[q, :, lanes] = value
            integral[q, :, lanes] += value * scale

        spatial_products(lambda r: deriv[r], kmat, mixed)
        for tile in range(2):
            spatial_mix(tile, (0, 3, 6), star, mixed, store)
        return scale

    lax.fori_loop(1, ORDER, degree, jnp.float32(1.0))

    for r in range(QUANT):
        traced = dot(proj[...], split3(integral[r]))
        for f in range(4):
            trace[pl.ds(r * ROWS, ROWS), pl.ds(f * ELEM, ELEM)] = traced[f * ROWS : (f + 1) * ROWS]
    trace[pl.ds(QUANT * ROWS, COMPS - QUANT * ROWS), :] = jnp.zeros((COMPS - QUANT * ROWS, COLS), f32)
    table[...] = split2(trace[...])
    column = iota((COLS, 256), 0)
    slots[...] = halves(dot(table[...], one_hot(column == face_at.astype(jnp.int32))))
    wire = dot(narrow(), split2(slots[...]))
    whole = code_at.astype(jnp.int32)
    partner = jnp.where(whole >= 0, whole + 1 - 2 * (whole % 2), -5).astype(f32)
    at = iota((WIRE, 256), 0)
    wire = jnp.where(at == CODE, code_at, jnp.where(at == PARTNER, partner, wire))
    put_packed(rows, wire[:128].T, jnp.concatenate([wire[128:], wire[128:]], axis=0).T)

    def remote(src, dst, send_sem, recv_sem, device):
        return pltpu.make_async_remote_copy(
            src_ref=src, dst_ref=dst, send_sem=send_sem, recv_sem=recv_sem, device_id=device, device_id_type=MESH
        )

    pl.semaphore_wait(barrier, 31 + 5)
    per = 32 // PIECES

    for piece in range(PIECES):
        def push(i, carry, piece=piece):
            o = lax.rem(own + i, 32)
            remote(rows.at[o], held.at[member, i], out_send, out_recv.at[piece], peer(o)).start()
            return carry

        lax.fori_loop(max(1, piece * per), (piece + 1) * per, push, 0)
    mine = pltpu.make_async_copy(rows.at[own], held.at[member, 0], local_sem)
    mine.start()

    sent = []

    def go(copy):
        copy.start()
        sent.append(copy)

    def part(m, piece):
        return held.at[m, pl.ds(piece * per, per)]

    def ring(m, piece, index, device):
        return remote(part(m, piece), part(m, piece), ring_send.at[index], ring_recv.at[index], device)

    def side(m, piece, index):
        return remote(part(m, piece), part(m, piece), side_send.at[index], side_recv.at[index], to_side)

    def own_piece(piece):
        count = per - 1 if piece == 0 else per
        got = held.at[member, pl.ds(piece * per, count)]
        remote(rows.at[pl.ds(0, count)], got, out_send, out_recv.at[piece], to_up).wait_recv()
        if piece == 0:
            mine.wait()
        go(ring(member, piece, piece, to_up))
        go(ring(member, piece, PIECES + piece, to_down))
        go(side(member, piece, piece))

    def ring_piece(piece):
        ring(mem_down, piece, piece, to_up).wait_recv()
        if piece % 2 == 0:
            go(ring(mem_down, piece, 2 * PIECES + piece, to_up))
        go(side(mem_down, piece, PIECES + piece))
        ring(mem_up, piece, PIECES + piece, to_down).wait_recv()
        if piece % 2 == 1:
            go(ring(mem_up, piece, 2 * PIECES + piece, to_down))
        go(side(mem_up, piece, 2 * PIECES + piece))

    def far_piece(piece):
        ring(mem_far, piece, 2 * PIECES + piece, to_up).wait_recv()
        go(side(mem_far, piece, 3 * PIECES + piece))

    def side_pieces(m, index):
        for piece in range(PIECES):
            side(m, piece, index * PIECES + piece).wait_recv()

    def halo_side(s):
        halo_out[s] = halves(dot(table[...], one_hot(column == send_ref[pl.ds(s, 1), :])))

    def own_neighbours(f):
        index = index_ref[pl.ds(f, 1), :]
        raw[:, pl.ds(f * ELEM, ELEM)] = halves(dot(table[...], one_hot(column == index)))

    def face_matrices(f):
        for r in range(QUANT):
            total = normals_ref[0, pl.ds(f, 1), :] * star[0, r]
            for d in range(1, 3):
                total += normals_ref[d, pl.ds(f, 1), :] * star[d, r]
            matrix[f, r] = 0.5 * total

    def keep_volume(q, lanes, value):
        volume[q, :, lanes] = value

    halo_side(0)
    low = remote(halo_out.at[0], halo_in.at[1], halo_send.at[0], halo_recv.at[1], lower)
    low.start()
    halo_side(1)
    high = remote(halo_out.at[1], halo_in.at[0], halo_send.at[1], halo_recv.at[0], upper)
    high.start()
    for i, row in enumerate(friction_params(code_at, region_ref, table_ref)):
        params[pl.ds(i, 1), :] = row
    own_piece(0)
    own_neighbours(0)
    own_piece(1)
    own_neighbours(1)
    own_piece(2)
    ring_piece(0)
    own_neighbours(2)
    own_piece(3)
    ring_piece(1)

    want = unpacked(held, member)[1][:, PARTNER - 128 : PARTNER - 127]

    def matched(m):
        first, second = unpacked(held, m)
        pick = one_hot(want == to_row(second[:, CODE - 128 : CODE - 127]))
        values = jnp.concatenate([first, second], axis=1)
        high_part = values.astype(bf16)
        low_part = (values - high_part.astype(f32)).astype(bf16)
        return dot(pick, high_part) + dot(pick, low_part)

    total = matched(member)
    ring_piece(2)
    own_neighbours(3)
    ring_piece(3)
    far_piece(0)
    total += matched(mem_down)
    far_piece(1)
    total += matched(mem_up)
    far_piece(2)
    side_pieces(slot(y, 1 - core), 0)
    total += matched(slot(y, 1 - core))
    far_piece(3)
    side_pieces(slot(down, 1 - core), 1)
    total += matched(slot(down, 1 - core))
    side_pieces(slot(up, 1 - core), 2)
    total += matched(slot(up, 1 - core))
    total += matched(mem_far)
    side_pieces(slot(far, 1 - core), 3)
    total += matched(slot(far, 1 - core))
    put_packed(replies, total[:, :128], total[:, 128:])

    def reply(i, carry):
        o = lax.rem(own + 32 - i, 32)
        remote(replies.at[i], back.at[own], back_send, back_recv, peer(o)).start()
        return carry

    lax.fori_loop(1, 32, reply, 0)
    mine = pltpu.make_async_copy(replies.at[0], back.at[own], local_sem)
    mine.start()

    for f in range(4):
        face_matrices(f)
    spatial_products(lambda r: integral[r], kmat, mixed)
    for tile in range(2):
        spatial_mix(tile, (0, 3, 6), star, mixed, keep_volume)

    remote(halo_out.at[1], halo_in.at[0], halo_send.at[1], halo_recv.at[0], upper).wait_recv()
    remote(halo_out.at[0], halo_in.at[1], halo_send.at[0], halo_recv.at[1], lower).wait_recv()
    halo = [split2(halo_in[0]), split2(halo_in[1])]
    first_row = iota((8, ELEM), 0) == 0
    for f in range(4):
        cols = pl.ds(f * ELEM, ELEM)
        index = index_ref[pl.ds(f, 1), :]
        near = dot(halo[0], one_hot(iota((256, ELEM), 0) + COLS == index))
        near += dot(halo[1], one_hot(iota((256, ELEM), 0) + (COLS + 256) == index))
        near = halves(near)
        orient = orient_ref[pl.ds(f, 1), :]
        turn = orient % 3
        reversed_face = orient >= 3
        for r in range(QUANT):
            at = [r * ROWS + 8 * g for g in range(3)]
            group = [raw[pl.ds(a, 8), cols] + near[a : a + 8] for a in at]
            moved = [
                jnp.where(turn == 0, group[g], jnp.where(turn == 1, group[(g + 1) % 3], group[(g + 2) % 3]))
                for g in range(3)
            ]
            for g in range(3):
                reverse = jnp.where(first_row, moved[(3 - g) % 3], flip(moved[(5 - g) % 3]))
                raw[pl.ds(at[g], 8), cols] = jnp.where(reversed_face, reverse, moved[g])
    outer = raw

    for copy in sent:
        copy.wait_send()
    low.wait_send()
    high.wait_send()
    out_done = remote(rows.at[pl.ds(0, 31)], held.at[member, pl.ds(0, 31)], out_send, out_recv.at[0], to_up)
    out_done.wait_send()
    face_col = to_col(face_at).astype(jnp.int32)
    mine.wait()
    returned = remote(replies.at[pl.ds(0, 31)], back.at[pl.ds(0, 31)], back_send, back_recv, to_up)
    returned.wait_send()
    returned.wait_recv()
    first, second = unpacked(back)
    other = dot(widen(), split2(jnp.concatenate([first.T, second.T[: WIRE - 128]], axis=0)))
    law = [params[pl.ds(i, 1), :] for i in range(3)]
    imposed = split2(
        jnp.concatenate(
            [friction(slots[...], other, code_at, law), jnp.zeros((COMPS - QUANT * ROWS, 256), f32)], axis=0
        )
    )

    for f in range(4):
        cols = pl.ds(f * ELEM, ELEM)
        put = face_col == iota((256, ELEM), 1) + f * ELEM
        fault = halves(dot(imposed, one_hot(put)))
        is_fault = jnp.sum(jnp.where(put, 1.0, 0.0), axis=0, keepdims=True) > 0.5
        outer[:, cols] = jnp.where(is_fault, fault, outer[:, cols])
        for tile in range(ELEM // 128):
            lanes = pl.ds(tile * 128, 128)
            cols = pl.ds(f * ELEM + tile * 128, 128)
            speed = 0.5 * speed_ref[:, lanes]
            for chunk in range(3):
                at = [pl.ds(r * ROWS + 8 * chunk, 8) for r in range(QUANT)]
                summed = [trace[at[t], cols] + outer[at[t], cols] for t in range(QUANT)]
                for r in range(QUANT):
                    flux = speed * (trace[at[r], cols] - outer[at[r], cols])
                    for t in range(QUANT):
                        flux += matrix[f, r, pl.ds(t, 1), lanes] * summed[t]
                    fluxes[r, pl.ds(f * ROWS + 8 * chunk, 8), lanes] = flux

    for r in range(QUANT):
        change_ref[r] = 0.25 * (volume[r] - dot(lift[...], split3(fluxes[r])))


def step(*operands):
    vmem, dma = pl.BlockSpec(memory_space=pltpu.VMEM), pltpu.SemaphoreType.DMA
    return pl.pallas_call(
        step_body,
        out_shape=jax.ShapeDtypeStruct((QUANT, BASIS, ELEM), f32),
        in_specs=[vmem] * 13 + [pl.BlockSpec(memory_space=pltpu.SMEM)],
        out_specs=vmem,
        scratch_shapes=[
            pltpu.VMEM((3, QUANT, QUANT, ELEM), f32),
            pltpu.VMEM((3 * BASIS, 3 * BASIS), bf16),
            pltpu.VMEM((4 * ROWS, 3 * BASIS), bf16),
            pltpu.VMEM((BASIS, 12 * ROWS), bf16),
            pltpu.VMEM((QUANT, 3 * BASIS, ELEM), f32),
            pltpu.VMEM((QUANT, BASIS, ELEM), f32),
            pltpu.VMEM((QUANT, BASIS, ELEM), f32),
            pltpu.VMEM((QUANT, BASIS, ELEM), f32),
            pltpu.VMEM((COMPS, COLS), f32),
            pltpu.VMEM((2 * COMPS, COLS), bf16),
            pltpu.VMEM((COMPS, 256), f32),
            pltpu.VMEM((COMPS, COLS), f32),
            pltpu.VMEM((4, QUANT, QUANT, ELEM), f32),
            pltpu.VMEM((QUANT, 4 * ROWS, ELEM), f32),
            pltpu.VMEM((2, 4, ROWS, BASIS), f32),
            pltpu.VMEM((8, 256), f32),
            pltpu.VMEM((32, 12, 128), f32),
            pltpu.VMEM((8, 32, 12, 128), f32),
            pltpu.VMEM((32, 12, 128), f32),
            pltpu.VMEM((32, 12, 128), f32),
            pltpu.VMEM((2, COMPS, 256), f32),
            pltpu.VMEM((2, COMPS, 256), f32),
            dma((2,)), dma((2,)), dma, dma((PIECES,)), dma((3 * PIECES,)), dma((3 * PIECES,)),
            dma((4 * PIECES,)), dma((4 * PIECES,)), dma, dma, dma,
        ],
        compiler_params=pltpu.CompilerParams(collective_id=0, has_side_effects=True, vmem_limit_bytes=VMEM_LIMIT),
    )(*operands)


def local(
    element_dofs, star_matrices, face_normals, wave_speed, stiffness, face_projection, face_lift, friction_table,
    neighbour_index, orientation, send_list, fault_face, fault_dest, fault_region,
):
    change = step(
        jnp.transpose(element_dofs, (1, 0, 2)),
        jnp.transpose(star_matrices, (1, 2, 0, 3)),
        jnp.transpose(stiffness, (1, 0, 2)).reshape(3 * BASIS, BASIS),
        jnp.transpose(face_projection, (1, 0, 2)),
        jnp.transpose(face_lift, (2, 0, 1)),
        face_normals, wave_speed.reshape(1, -1), neighbour_index, orientation, send_list,
        fault_face.reshape(1, -1), fault_dest.reshape(1, -1), fault_region.reshape(1, -1), friction_table,
    )
    return element_dofs + jnp.transpose(change, (1, 0, 2))


def solution(mesh):
    return jax.shard_map(
        local,
        mesh=mesh,
        in_specs=(
            P(None, None, ("dom", "quad")),
            P(None, None, None, ("dom", "quad")),
            P(None, None, ("dom", "quad")),
            P(("dom", "quad")),
            P(),
            P(),
            P(),
            P(),
            P(None, ("dom", "quad")),
            P(None, ("dom", "quad")),
            P(None, ("dom", "quad")),
            P(("dom", "quad")),
            P(("dom", "quad")),
            P(),
        ),
        out_specs=P(None, None, ("dom", "quad")),
        check_vma=False,
    )
```

```python
import functools
import math

import jax
import jax.numpy as jnp
from jax import lax
from jax.experimental import pallas as pl
from jax.experimental.pallas import tpu as pltpu
from jax.sharding import PartitionSpec as P

ORDER = 6
NEWTON = 8
BASIS = 56
QUANT = 9
ELEM = 256
COLS = 4 * ELEM
ROWS = 24
COMPS = 224
WIRE = 192
CODE, PARTNER = 189, 190
PIECES = 4
DIRECT = (3,)
OFFSETS = [(dz, dx) for dz in (0, 1, 7, 2, 6, 3, 5, 4) for dx in (0, 1, 3, 2)]
f32, bf16 = jnp.float32, jnp.bfloat16
MESH = pl.DeviceIdType.MESH
VMEM_LIMIT = 32 * 1024 * 1024


def iota(shape, dim):
    return lax.broadcasted_iota(jnp.int32, shape, dim)


def one_hot(mask):
    return jnp.where(mask, 1.0, 0.0).astype(bf16)


def split2(x):
    high = x.astype(bf16).astype(f32)
    return jnp.concatenate([high, x - high], axis=0).astype(bf16)


def split3(x):
    high = x.astype(bf16).astype(f32)
    return jnp.concatenate([high, x - high, high], axis=0).astype(bf16)


def dot(a, b):
    return jnp.dot(a, b, preferred_element_type=f32)


def halves(x):
    n = x.shape[0] // 2
    return x[:n] + x[n:]


def to_col(row):
    n = row.shape[1]
    eye = iota((n, n), 0) == iota((n, n), 1)
    return jnp.sum(jnp.where(eye, row, 0.0), axis=1, keepdims=True)


def to_row(col):
    n = col.shape[0]
    eye = iota((n, n), 0) == iota((n, n), 1)
    return jnp.sum(jnp.where(eye, col, 0.0), axis=0, keepdims=True)


def slot_rows(dest, face):
    n = dest.shape[1]
    live = dest >= 0
    owner = jnp.where(live, dest // 1024, 64).astype(f32)
    code = jnp.where(live, dest % 1024, -1).astype(f32)
    owner_col = to_col(owner)
    earlier = (owner_col == owner) & (iota((n, n), 0) < iota((n, n), 1))
    rank = jnp.sum(jnp.where(earlier, 1.0, 0.0), axis=0, keepdims=True)
    place = jnp.where(live, owner * 8.0 + rank, -1.0)
    put = to_col(place) == iota((n, n), 1).astype(f32)
    face_at = jnp.sum(jnp.where(put, to_col(face.astype(f32) + 1.0), 0.0), axis=0, keepdims=True)
    code_at = jnp.sum(jnp.where(put, to_col(code + 1.0), 0.0), axis=0, keepdims=True)
    return face_at - 1.0, code_at - 1.0


def packed(first, second):
    swapped = pltpu.roll(pltpu.roll(second, 64, 1), 252, 0)
    pairs = jnp.where(iota((256, 128), 1) < 64, second, swapped)
    return first.reshape(32, 8, 128), pairs.reshape(32, 8, 128)[:, :4, :]


def put_packed(ref, first, second):
    ref[:, pl.ds(0, 8), :], ref[:, pl.ds(8, 4), :] = packed(first, second)


def unpacked(ref, *at):
    first = ref[(*at, slice(None), pl.ds(0, 8), slice(None))].reshape(256, 128)
    pairs = ref[(*at, slice(None), pl.ds(8, 4), slice(None))]
    pairs = jnp.concatenate([pairs, pairs], axis=1).reshape(256, 128)
    second = jnp.where(iota((256, 128), 0) % 8 < 4, pairs, pltpu.roll(pairs, 64, 1))
    return first, second


def narrow():
    value, row = iota((WIRE, 2 * COMPS), 0), iota((WIRE, 2 * COMPS), 1)
    row = jnp.where(row >= COMPS, row - COMPS, row)
    return one_hot((row == value + ((value * 9363) >> 16)) & (value < CODE))


def widen():
    row, value = iota((COMPS, 2 * WIRE), 0), iota((COMPS, 2 * WIRE), 1)
    value = jnp.where(value >= WIRE, value - WIRE, value)
    return one_hot((row == value + ((value * 9363) >> 16)) & (value < CODE))


def weight_parts(weights):
    high = weights.astype(bf16).astype(f32)
    return jnp.concatenate([high, high, weights - high], axis=1).astype(bf16)


def spatial_products(load, kmat_ref, mixed):
    for r in range(QUANT):
        mixed[r] = dot(kmat_ref[...], split3(load(r)))


def spatial_mix(tile, firsts, star_ref, mixed, store):
    lanes = pl.ds(tile * 128, 128)
    for first in firsts:
        total = [None] * 3
        for d in range(3):
            for r in range(QUANT):
                value = mixed[r, pl.ds(d * BASIS, BASIS), lanes]
                for i in range(3):
                    term = star_ref[d, first + i, pl.ds(r, 1), lanes] * value
                    total[i] = term if total[i] is None else total[i] + term
        for i in range(3):
            store(first + i, lanes, total[i])


def inverse_sinh(value):
    magnitude = jnp.abs(value)
    result = jnp.log(magnitude + jnp.sqrt(1.0 + magnitude * magnitude))
    return jnp.where(value < 0.0, -result, result)


def friction_params(code_at, region_ref, table_ref):
    code_col = to_col(code_at).astype(jnp.int32)
    pairs = region_ref.shape[1] // 32
    regions = jnp.concatenate(
        [jnp.broadcast_to(region_ref[:, pl.ds(o * pairs, pairs)], (8, pairs)) for o in range(32)], axis=0
    ).astype(f32)
    hit = (code_col // 2 == iota((256, pairs), 1)) & (code_col >= 0)
    region = to_row(jnp.sum(jnp.where(hit, regions, 0.0), axis=1, keepdims=True))
    params = []
    for row in range(3):
        value = jnp.full((1, 256), table_ref[row, 0], f32)
        for j in range(1, 8):
            value = jnp.where(region == float(j), table_ref[row, j], value)
        params.append(value)
    return params


def friction(own, other, code_at, params):
    rate_term, state_term, shear = params
    background = 3.0 * shear

    def comp(x, r):
        return x[r * ROWS : (r + 1) * ROWS]

    second = (code_at.astype(jnp.int32) % 2) == 1
    sign = jnp.where(second, -1.0, 1.0)
    pressure = 1.0 + jax.nn.softplus(2.0 - 0.5 * (comp(own, 0) + comp(other, 0)))
    locked = (
        0.5 * (comp(own, 3) + comp(other, 3)) + 0.5 * sign * (comp(other, 7) - comp(own, 7)) + background
    )
    stiff_rate = 0.5 * jnp.exp(state_term / rate_term)
    slip = jnp.zeros_like(locked)
    for _ in range(NEWTON):
        argument = stiff_rate * slip
        mismatch = 0.5 * slip + pressure * rate_term * inverse_sinh(argument) - locked
        gradient = 0.5 + pressure * rate_term * stiff_rate / jnp.sqrt(1.0 + argument * argument)
        slip = slip - 0.4 * mismatch / gradient
    third = 2.0 * (locked - 0.5 * slip - background) - comp(own, 3)
    seventh = comp(other, 7) - sign * slip
    return jnp.concatenate(
        [other[: 3 * ROWS], third, other[4 * ROWS : 7 * ROWS], seventh, other[8 * ROWS : QUANT * ROWS]], axis=0
    )


def flip(x):
    index = 7 - iota((8, 128), 0)
    parts = [
        jnp.take_along_axis(x[:, c : c + 128], index, axis=0, mode="promise_in_bounds") for c in range(0, x.shape[1], 128)
    ]
    return jnp.concatenate(parts, axis=1)


def step_body(
    x_ref, star_in, stiff_ref, proj_in, lift_in, normals_ref, speed_ref, index_ref, orient_ref, send_ref, face_ref,
    dest_ref, region_ref, table_ref,
    updated_ref,
    star, kmat, proj, lift, mixed, deriv, integral, volume, trace, table, slots, raw, matrix, fluxes, points, params,
    rows, held, replies, back, halo_out, halo_in,
    halo_send, halo_recv, out_send, out_recv, ring_send, ring_recv, side_send, side_recv, back_send, back_recv, local_sem,
):
    dom, quad = lax.axis_index("dom"), lax.axis_index("quad")
    doms = lax.axis_size("dom")
    block, member = dom // 8, dom % 8
    y, core = member // 2, member % 2
    own = block * 4 + quad

    def slot(yy, cc):
        return yy * 2 + cc

    def peer(i, sign):
        dz, dx = OFFSETS[i]
        zz, xx = lax.rem(block + (8 + sign * dz) % 8, 8), lax.rem(quad + (4 + sign * dx) % 4, 4)
        return zz * 4 + xx, (zz * 8 + member, xx)

    up, down, far = (y + 1) % 4, (y + 3) % 4, (y + 2) % 4
    mem_up, mem_down, mem_far = slot(up, core), slot(down, core), slot(far, core)
    to_up, to_down = (block * 8 + mem_up, quad), (block * 8 + mem_down, quad)
    to_far = (block * 8 + mem_far, quad)
    to_side = (block * 8 + slot(y, 1 - core), quad)
    upper, lower = (lax.rem(dom + 1, doms), quad), (lax.rem(dom + doms - 1, doms), quad)

    barrier = pltpu.get_barrier_semaphore()

    for i in range(31, 0, -1):
        pl.semaphore_signal(barrier, inc=1, device_id=peer(i, -1)[1], device_id_type=MESH)
    for device in (to_up, to_down, to_side, to_far, upper, lower):
        pl.semaphore_signal(barrier, inc=1, device_id=device, device_id_type=MESH)

    for q in range(QUANT):
        for r in range(QUANT):
            star[:, q, r, :] = star_in[q, r]
    kmat[...] = weight_parts(stiff_ref[...])
    for source, padded in ((proj_in, points.at[0]), (lift_in, points.at[1])):
        padded[...] = jnp.zeros_like(padded)
        for p in range(21):
            padded[:, p // 7 * 8 + p % 7, :] = source[p]
    proj[...] = weight_parts(points[0].reshape(4 * ROWS, BASIS))
    lift[...] = weight_parts(
        jnp.concatenate(
            [
                jnp.concatenate([points[1].reshape(4 * ROWS, BASIS), jnp.zeros((4 * ROWS, 128 - BASIS), f32)], axis=1),
                jnp.zeros((128 - 4 * ROWS, 128), f32),
            ],
            axis=0,
        ).T[:BASIS, : 4 * ROWS]
    )
    face_at, code_at = slot_rows(dest_ref[...], face_ref[...])

    for r in range(QUANT):
        value = x_ref[r]
        deriv[r] = value
        integral[r] = value

    def degree(k, scale):
        scale = scale / (k + 1)

        def store(q, lanes, value):
            deriv[q, :, lanes] = value
            integral[q, :, lanes] += value * scale

        spatial_products(lambda r: deriv[r], kmat, mixed)
        for tile in range(2):
            spatial_mix(tile, (0, 3, 6), star, mixed, store)
        return scale

    scale = 1.0
    for k in range(1, ORDER):
        scale = degree(k, scale)

    for r in range(QUANT):
        traced = dot(proj[...], split3(integral[r]))
        for f in range(4):
            trace[pl.ds(r * ROWS, ROWS), pl.ds(f * ELEM, ELEM)] = traced[f * ROWS : (f + 1) * ROWS]
    trace[pl.ds(QUANT * ROWS, COMPS - QUANT * ROWS), :] = jnp.zeros((COMPS - QUANT * ROWS, COLS), f32)
    table[...] = split2(trace[...])
    column = iota((COLS, 256), 0)
    slots[...] = halves(dot(table[...], one_hot(column == face_at.astype(jnp.int32))))
    wire = dot(narrow(), split2(slots[...]))
    whole = code_at.astype(jnp.int32)
    partner = jnp.where(whole >= 0, whole + 1 - 2 * (whole % 2), -5).astype(f32)
    at = iota((WIRE, 256), 0)
    wire = jnp.where(at == CODE, code_at, jnp.where(at == PARTNER, partner, wire))
    put_packed(rows, wire[:128].T, jnp.concatenate([wire[128:], wire[128:]], axis=0).T)

    def remote(src, dst, send_sem, recv_sem, device):
        return pltpu.make_async_remote_copy(
            src_ref=src, dst_ref=dst, send_sem=send_sem, recv_sem=recv_sem, device_id=device, device_id_type=MESH
        )

    pl.semaphore_wait(barrier, 31 + 6)
    per = 32 // PIECES

    for i in range(31, 0, -1):
        o, device = peer(i, 1)
        remote(rows.at[o], held.at[member, i], out_send, out_recv.at[i // per], device).start()
    mine = pltpu.make_async_copy(rows.at[own], held.at[member, 0], local_sem)
    mine.start()

    sent = []

    def go(copy):
        copy.start()
        sent.append(copy)

    def part(m, piece):
        return held.at[m, pl.ds(piece * per, per)]

    def ring(m, piece, index, device):
        return remote(part(m, piece), part(m, piece), ring_send.at[index], ring_recv.at[index], device)

    def side(m, piece, index):
        return remote(part(m, piece), part(m, piece), side_send.at[index], side_recv.at[index], to_side)

    def own_piece(piece):
        count = per - 1 if piece == 0 else per
        got = held.at[member, pl.ds(piece * per, count)]
        remote(rows.at[pl.ds(0, count)], got, out_send, out_recv.at[piece], to_up).wait_recv()
        if piece == 0:
            mine.wait()
        go(ring(member, piece, piece, to_up))
        go(ring(member, piece, PIECES + piece, to_down))
        go(side(member, piece, piece))
        if piece in DIRECT:
            go(ring(member, piece, 2 * PIECES + piece, to_far))

    def ring_piece(piece):
        ring(mem_down, piece, piece, to_up).wait_recv()
        if piece % 2 == 0 and piece not in DIRECT:
            go(ring(mem_down, piece, 2 * PIECES + piece, to_up))
        go(side(mem_down, piece, PIECES + piece))
        ring(mem_up, piece, PIECES + piece, to_down).wait_recv()
        if piece % 2 == 1 and piece not in DIRECT:
            go(ring(mem_up, piece, 2 * PIECES + piece, to_down))
        go(side(mem_up, piece, 2 * PIECES + piece))

    def far_piece(piece):
        ring(mem_far, piece, 2 * PIECES + piece, to_up).wait_recv()
        go(side(mem_far, piece, 3 * PIECES + piece))

    def side_pieces(m, index):
        for piece in range(PIECES):
            side(m, piece, index * PIECES + piece).wait_recv()

    def halo_side(s):
        halo_out[s] = halves(dot(table[...], one_hot(column == send_ref[pl.ds(s, 1), :])))

    def own_neighbours(f):
        index = index_ref[pl.ds(f, 1), :]
        raw[:, pl.ds(f * ELEM, ELEM)] = halves(dot(table[...], one_hot(column == index)))

    def face_matrices(f):
        for r in range(QUANT):
            total = normals_ref[0, pl.ds(f, 1), :] * star[0, r]
            for d in range(1, 3):
                total += normals_ref[d, pl.ds(f, 1), :] * star[d, r]
            matrix[f, r] = 0.5 * total

    def keep_volume(q, lanes, value):
        volume[q, :, lanes] = value

    halo_side(0)
    low = remote(halo_out.at[0], halo_in.at[1], halo_send.at[0], halo_recv.at[1], lower)
    low.start()
    halo_side(1)
    high = remote(halo_out.at[1], halo_in.at[0], halo_send.at[1], halo_recv.at[0], upper)
    high.start()
    for i, row in enumerate(friction_params(code_at, region_ref, table_ref)):
        params[pl.ds(i, 1), :] = row
    def wanted():
        return unpacked(held, member)[1][:, PARTNER - 128 : PARTNER - 127]

    def matched(m, want):
        first, second = unpacked(held, m)
        pick = one_hot(want == to_row(second[:, CODE - 128 : CODE - 127]))
        values = jnp.concatenate([first, second], axis=1)
        high_part = values.astype(bf16)
        low_part = (values - high_part.astype(f32)).astype(bf16)
        return dot(pick, high_part) + dot(pick, low_part)

    own_neighbours(0)
    own_piece(0)
    own_neighbours(1)
    own_piece(1)
    own_neighbours(2)
    own_piece(2)
    own_neighbours(3)
    ring_piece(0)
    own_piece(3)
    ring_piece(1)
    want = wanted()
    total = matched(member, want)
    ring_piece(2)
    far_piece(0)
    ring_piece(3)
    total += matched(mem_down, want)
    total += matched(mem_up, want)
    side_pieces(slot(y, 1 - core), 0)
    total += matched(slot(y, 1 - core), want)
    for piece in range(1, PIECES):
        far_piece(piece)
    side_pieces(slot(down, 1 - core), 1)
    total += matched(slot(down, 1 - core), want)
    side_pieces(slot(up, 1 - core), 2)
    total += matched(slot(up, 1 - core), want)
    total += matched(mem_far, want)
    side_pieces(slot(far, 1 - core), 3)
    total += matched(slot(far, 1 - core), want)
    put_packed(replies, total[:, :128], total[:, 128:])

    for i in range(31, 0, -1):
        remote(replies.at[i], back.at[own], back_send, back_recv, peer(i, -1)[1]).start()
    mine = pltpu.make_async_copy(replies.at[0], back.at[own], local_sem)
    mine.start()

    for f in range(4):
        face_matrices(f)
    spatial_products(lambda r: integral[r], kmat, mixed)
    for tile in range(2):
        spatial_mix(tile, (0, 3, 6), star, mixed, keep_volume)

    remote(halo_out.at[1], halo_in.at[0], halo_send.at[1], halo_recv.at[0], upper).wait_recv()
    remote(halo_out.at[0], halo_in.at[1], halo_send.at[0], halo_recv.at[1], lower).wait_recv()
    halo = [split2(halo_in[0]), split2(halo_in[1])]
    first_row = iota((8, ELEM), 0) == 0
    for f in range(4):
        cols = pl.ds(f * ELEM, ELEM)
        index = index_ref[pl.ds(f, 1), :]
        near = dot(halo[0], one_hot(iota((256, ELEM), 0) + COLS == index))
        near += dot(halo[1], one_hot(iota((256, ELEM), 0) + (COLS + 256) == index))
        near = halves(near)
        orient = orient_ref[pl.ds(f, 1), :]
        turn = orient % 3
        reversed_face = orient >= 3
        for r in range(QUANT):
            at = [r * ROWS + 8 * g for g in range(3)]
            group = [raw[pl.ds(a, 8), cols] + near[a : a + 8] for a in at]
            moved = [
                jnp.where(turn == 0, group[g], jnp.where(turn == 1, group[(g + 1) % 3], group[(g + 2) % 3]))
                for g in range(3)
            ]
            for g in range(3):
                reverse = jnp.where(first_row, moved[(3 - g) % 3], flip(moved[(5 - g) % 3]))
                raw[pl.ds(at[g], 8), cols] = jnp.where(reversed_face, reverse, moved[g])
    outer = raw

    for copy in sent:
        copy.wait_send()
    low.wait_send()
    high.wait_send()
    out_done = remote(rows.at[pl.ds(0, 31)], held.at[member, pl.ds(0, 31)], out_send, out_recv.at[0], to_up)
    out_done.wait_send()
    face_col = to_col(face_at).astype(jnp.int32)
    mine.wait()
    returned = remote(replies.at[pl.ds(0, 31)], back.at[pl.ds(0, 31)], back_send, back_recv, to_up)
    returned.wait_send()
    returned.wait_recv()
    first, second = unpacked(back)
    other = dot(widen(), split2(jnp.concatenate([first.T, second.T[: WIRE - 128]], axis=0)))
    law = [params[pl.ds(i, 1), :] for i in range(3)]
    imposed = split2(
        jnp.concatenate(
            [friction(slots[...], other, code_at, law), jnp.zeros((COMPS - QUANT * ROWS, 256), f32)], axis=0
        )
    )

    for f in range(4):
        cols = pl.ds(f * ELEM, ELEM)
        put = face_col == iota((256, ELEM), 1) + f * ELEM
        fault = halves(dot(imposed, one_hot(put)))
        is_fault = jnp.sum(jnp.where(put, 1.0, 0.0), axis=0, keepdims=True) > 0.5
        outer[:, cols] = jnp.where(is_fault, fault, outer[:, cols])
        for tile in range(ELEM // 128):
            lanes = pl.ds(tile * 128, 128)
            cols = pl.ds(f * ELEM + tile * 128, 128)
            speed = 0.5 * speed_ref[:, lanes]
            for chunk in range(3):
                at = [pl.ds(r * ROWS + 8 * chunk, 8) for r in range(QUANT)]
                summed = [trace[at[t], cols] + outer[at[t], cols] for t in range(QUANT)]
                for r in range(QUANT):
                    flux = speed * (trace[at[r], cols] - outer[at[r], cols])
                    for t in range(QUANT):
                        flux += matrix[f, r, pl.ds(t, 1), lanes] * summed[t]
                    fluxes[r, pl.ds(f * ROWS + 8 * chunk, 8), lanes] = flux

    for r in range(QUANT):
        updated_ref[r] = x_ref[r] + 0.25 * (volume[r] - dot(lift[...], split3(fluxes[r])))


def step(*operands):
    vmem, dma = pl.BlockSpec(memory_space=pltpu.VMEM), pltpu.SemaphoreType.DMA
    return pl.pallas_call(
        step_body,
        out_shape=jax.ShapeDtypeStruct((QUANT, BASIS, ELEM), f32),
        in_specs=[vmem] * 13 + [pl.BlockSpec(memory_space=pltpu.SMEM)],
        out_specs=vmem,
        scratch_shapes=[
            pltpu.VMEM((3, QUANT, QUANT, ELEM), f32),
            pltpu.VMEM((3 * BASIS, 3 * BASIS), bf16),
            pltpu.VMEM((4 * ROWS, 3 * BASIS), bf16),
            pltpu.VMEM((BASIS, 12 * ROWS), bf16),
            pltpu.VMEM((QUANT, 3 * BASIS, ELEM), f32),
            pltpu.VMEM((QUANT, BASIS, ELEM), f32),
            pltpu.VMEM((QUANT, BASIS, ELEM), f32),
            pltpu.VMEM((QUANT, BASIS, ELEM), f32),
            pltpu.VMEM((COMPS, COLS), f32),
            pltpu.VMEM((2 * COMPS, COLS), bf16),
            pltpu.VMEM((COMPS, 256), f32),
            pltpu.VMEM((COMPS, COLS), f32),
            pltpu.VMEM((4, QUANT, QUANT, ELEM), f32),
            pltpu.VMEM((QUANT, 4 * ROWS, ELEM), f32),
            pltpu.VMEM((2, 4, ROWS, BASIS), f32),
            pltpu.VMEM((8, 256), f32),
            pltpu.VMEM((32, 12, 128), f32),
            pltpu.VMEM((8, 32, 12, 128), f32),
            pltpu.VMEM((32, 12, 128), f32),
            pltpu.VMEM((32, 12, 128), f32),
            pltpu.VMEM((2, COMPS, 256), f32),
            pltpu.VMEM((2, COMPS, 256), f32),
            dma((2,)), dma((2,)), dma, dma((PIECES,)), dma((3 * PIECES,)), dma((3 * PIECES,)),
            dma((4 * PIECES,)), dma((4 * PIECES,)), dma, dma, dma,
        ],
        compiler_params=pltpu.CompilerParams(collective_id=0, has_side_effects=True, vmem_limit_bytes=VMEM_LIMIT),
    )(*operands)


def local(
    element_dofs, star_matrices, face_normals, wave_speed, stiffness, face_projection, face_lift, friction_table,
    neighbour_index, orientation, send_list, fault_face, fault_dest, fault_region,
):
    updated = step(
        jnp.transpose(element_dofs, (1, 0, 2)),
        jnp.transpose(star_matrices, (1, 2, 0, 3)),
        jnp.transpose(stiffness, (1, 0, 2)).reshape(3 * BASIS, BASIS),
        jnp.transpose(face_projection, (1, 0, 2)),
        jnp.transpose(face_lift, (2, 0, 1)),
        face_normals, wave_speed.reshape(1, -1), neighbour_index, orientation, send_list,
        fault_face.reshape(1, -1), fault_dest.reshape(1, -1), fault_region.reshape(1, -1), friction_table,
    )
    return jnp.transpose(updated, (1, 0, 2))


def solution(mesh):
    return jax.shard_map(
        local,
        mesh=mesh,
        in_specs=(
            P(None, None, ("dom", "quad")),
            P(None, None, None, ("dom", "quad")),
            P(None, None, ("dom", "quad")),
            P(("dom", "quad")),
            P(),
            P(),
            P(),
            P(),
            P(None, ("dom", "quad")),
            P(None, ("dom", "quad")),
            P(None, ("dom", "quad")),
            P(("dom", "quad")),
            P(("dom", "quad")),
            P(),
        ),
        out_specs=P(None, None, ("dom", "quad")),
        check_vma=False,
    )
```

```python
import functools
import math

import jax
import jax.numpy as jnp
from jax import lax
from jax.experimental import pallas as pl
from jax.experimental.pallas import tpu as pltpu
from jax.sharding import PartitionSpec as P

ORDER = 6
NEWTON = 8
BASIS = 56
QUANT = 9
ELEM = 256
COLS = 4 * ELEM
ROWS = 24
COMPS = 224
WIRE = 192
CODE, PARTNER = 189, 190
PIECES = 4
DIRECT = (3,)
OFFSETS = [(dz, dx) for dz in (0, 1, 7, 2, 6, 3, 5, 4) for dx in (0, 1, 3, 2)]
f32, bf16 = jnp.float32, jnp.bfloat16
MESH = pl.DeviceIdType.MESH
VMEM_LIMIT = 56 * 1024 * 1024


def iota(shape, dim):
    return lax.broadcasted_iota(jnp.int32, shape, dim)


def one_hot(mask):
    return jnp.where(mask, 1.0, 0.0).astype(bf16)


def split2(x):
    high = x.astype(bf16).astype(f32)
    return jnp.concatenate([high, x - high], axis=0).astype(bf16)


def split3(x):
    high = x.astype(bf16).astype(f32)
    return jnp.concatenate([high, x - high, high], axis=0).astype(bf16)


def dot(a, b):
    return jnp.dot(a, b, preferred_element_type=f32)


def halves(x):
    n = x.shape[0] // 2
    return x[:n] + x[n:]


def to_col(row):
    n = row.shape[1]
    eye = iota((n, n), 0) == iota((n, n), 1)
    return jnp.sum(jnp.where(eye, row, 0.0), axis=1, keepdims=True)


def to_row(col):
    n = col.shape[0]
    eye = iota((n, n), 0) == iota((n, n), 1)
    return jnp.sum(jnp.where(eye, col, 0.0), axis=0, keepdims=True)


def slot_rows(dest, face):
    n = dest.shape[1]
    live = dest >= 0
    owner = jnp.where(live, dest // 1024, 64).astype(f32)
    code = jnp.where(live, dest % 1024, -1).astype(f32)
    owner_col = to_col(owner)
    earlier = (owner_col == owner) & (iota((n, n), 0) < iota((n, n), 1))
    rank = jnp.sum(jnp.where(earlier, 1.0, 0.0), axis=0, keepdims=True)
    place = jnp.where(live, owner * 8.0 + rank, -1.0)
    put = to_col(place) == iota((n, n), 1).astype(f32)
    face_at = jnp.sum(jnp.where(put, to_col(face.astype(f32) + 1.0), 0.0), axis=0, keepdims=True)
    code_at = jnp.sum(jnp.where(put, to_col(code + 1.0), 0.0), axis=0, keepdims=True)
    return face_at - 1.0, code_at - 1.0


def packed(first, second):
    swapped = pltpu.roll(pltpu.roll(second, 64, 1), 252, 0)
    pairs = jnp.where(iota((256, 128), 1) < 64, second, swapped)
    return first.reshape(32, 8, 128), pairs.reshape(32, 8, 128)[:, :4, :]


def put_packed(ref, first, second):
    ref[:, pl.ds(0, 8), :], ref[:, pl.ds(8, 4), :] = packed(first, second)


def unpacked(ref, *at):
    first = ref[(*at, slice(None), pl.ds(0, 8), slice(None))].reshape(256, 128)
    pairs = ref[(*at, slice(None), pl.ds(8, 4), slice(None))]
    pairs = jnp.concatenate([pairs, pairs], axis=1).reshape(256, 128)
    second = jnp.where(iota((256, 128), 0) % 8 < 4, pairs, pltpu.roll(pairs, 64, 1))
    return first, second


def narrow():
    value, row = iota((WIRE, 2 * COMPS), 0), iota((WIRE, 2 * COMPS), 1)
    row = jnp.where(row >= COMPS, row - COMPS, row)
    return one_hot((row == value + ((value * 9363) >> 16)) & (value < CODE))


def widen():
    row, value = iota((COMPS, 2 * WIRE), 0), iota((COMPS, 2 * WIRE), 1)
    value = jnp.where(value >= WIRE, value - WIRE, value)
    return one_hot((row == value + ((value * 9363) >> 16)) & (value < CODE))


def weight_parts(weights):
    high = weights.astype(bf16).astype(f32)
    return jnp.concatenate([high, high, weights - high], axis=1).astype(bf16)


def spatial_products(load, kmat_ref, mixed):
    for r in range(QUANT):
        mixed[r] = dot(kmat_ref[...], split3(load(r)))


def spatial_mix(tile, firsts, star_ref, mixed, store):
    lanes = pl.ds(tile * 128, 128)
    for first in firsts:
        total = [None] * 3
        for d in range(3):
            for r in range(QUANT):
                value = mixed[r, pl.ds(d * BASIS, BASIS), lanes]
                for i in range(3):
                    term = star_ref[d, first + i, pl.ds(r, 1), lanes] * value
                    total[i] = term if total[i] is None else total[i] + term
        for i in range(3):
            store(first + i, lanes, total[i])


def inverse_sinh(value):
    magnitude = jnp.abs(value)
    result = jnp.log(magnitude + jnp.sqrt(1.0 + magnitude * magnitude))
    return jnp.where(value < 0.0, -result, result)


def friction_params(code_at, region_ref, table_ref):
    code_col = to_col(code_at).astype(jnp.int32)
    pairs = region_ref.shape[1] // 32
    regions = jnp.concatenate(
        [jnp.broadcast_to(region_ref[:, pl.ds(o * pairs, pairs)], (8, pairs)) for o in range(32)], axis=0
    ).astype(f32)
    hit = (code_col // 2 == iota((256, pairs), 1)) & (code_col >= 0)
    region = to_row(jnp.sum(jnp.where(hit, regions, 0.0), axis=1, keepdims=True))
    params = []
    for row in range(3):
        value = jnp.full((1, 256), table_ref[row, 0], f32)
        for j in range(1, 8):
            value = jnp.where(region == float(j), table_ref[row, j], value)
        params.append(value)
    return params


def friction(own, other, code_at, params):
    rate_term, state_term, shear = params
    background = 3.0 * shear

    def comp(x, r):
        return x[r * ROWS : (r + 1) * ROWS]

    second = (code_at.astype(jnp.int32) % 2) == 1
    sign = jnp.where(second, -1.0, 1.0)
    pressure = 1.0 + jax.nn.softplus(2.0 - 0.5 * (comp(own, 0) + comp(other, 0)))
    locked = (
        0.5 * (comp(own, 3) + comp(other, 3)) + 0.5 * sign * (comp(other, 7) - comp(own, 7)) + background
    )
    stiff_rate = 0.5 * jnp.exp(state_term / rate_term)
    slip = jnp.zeros_like(locked)
    for _ in range(NEWTON):
        argument = stiff_rate * slip
        mismatch = 0.5 * slip + pressure * rate_term * inverse_sinh(argument) - locked
        gradient = 0.5 + pressure * rate_term * stiff_rate / jnp.sqrt(1.0 + argument * argument)
        slip = slip - 0.4 * mismatch / gradient
    third = 2.0 * (locked - 0.5 * slip - background) - comp(own, 3)
    seventh = comp(other, 7) - sign * slip
    return jnp.concatenate(
        [other[: 3 * ROWS], third, other[4 * ROWS : 7 * ROWS], seventh, other[8 * ROWS : QUANT * ROWS]], axis=0
    )


def flip(x):
    index = 7 - iota((8, 128), 0)
    parts = [
        jnp.take_along_axis(x[:, c : c + 128], index, axis=0, mode="promise_in_bounds") for c in range(0, x.shape[1], 128)
    ]
    return jnp.concatenate(parts, axis=1)


def step_body(*refs):
    sources, refs = refs[:14], refs[14:]
    copied, refs = refs[-14:], refs[:-14]
    (
        x_ref, star_in, stiff_ref, proj_in, lift_in, normals_ref, speed_ref, index_ref,
        orient_ref, send_ref, face_ref, dest_ref, region_ref, table_ref,
    ) = copied
    (
        updated_ref,
        star, kmat, proj, lift, mixed, deriv, integral, volume, trace, table, slots, raw, matrix, fluxes, points, params,
        rows, held, replies, back, halo_out, halo_in,
        halo_send, halo_recv, out_send, out_recv, ring_send, ring_recv, side_send, side_recv, back_send, back_recv, local_sem, in_sem,
    ) = refs
    dom, quad = lax.axis_index("dom"), lax.axis_index("quad")
    doms = lax.axis_size("dom")
    block, member = dom // 8, dom % 8
    y, core = member // 2, member % 2
    own = block * 4 + quad

    def slot(yy, cc):
        return yy * 2 + cc

    def peer(i, sign):
        dz, dx = OFFSETS[i]
        zz, xx = lax.rem(block + (8 + sign * dz) % 8, 8), lax.rem(quad + (4 + sign * dx) % 4, 4)
        return zz * 4 + xx, (zz * 8 + member, xx)

    up, down, far = (y + 1) % 4, (y + 3) % 4, (y + 2) % 4
    mem_up, mem_down, mem_far = slot(up, core), slot(down, core), slot(far, core)
    to_up, to_down = (block * 8 + mem_up, quad), (block * 8 + mem_down, quad)
    to_far = (block * 8 + mem_far, quad)
    to_side = (block * 8 + slot(y, 1 - core), quad)
    upper, lower = (lax.rem(dom + 1, doms), quad), (lax.rem(dom + doms - 1, doms), quad)

    arriving = [pltpu.make_async_copy(source, held_in, in_sem.at[i]) for i, (source, held_in) in enumerate(zip(sources, copied))]
    for copy in arriving:
        copy.start()

    barrier = pltpu.get_barrier_semaphore()

    for i in range(31, 0, -1):
        pl.semaphore_signal(barrier, inc=1, device_id=peer(i, -1)[1], device_id_type=MESH)
    for device in (to_up, to_down, to_side, to_far, upper, lower):
        pl.semaphore_signal(barrier, inc=1, device_id=device, device_id_type=MESH)

    for copy in arriving:
        copy.wait()
    for q in range(QUANT):
        for r in range(QUANT):
            star[:, q, r, :] = star_in[q, r]
    kmat[...] = weight_parts(stiff_ref[...])
    for source, padded in ((proj_in, points.at[0]), (lift_in, points.at[1])):
        padded[...] = jnp.zeros_like(padded)
        for p in range(21):
            padded[:, p // 7 * 8 + p % 7, :] = source[p]
    proj[...] = weight_parts(points[0].reshape(4 * ROWS, BASIS))
    lift[...] = weight_parts(
        jnp.concatenate(
            [
                jnp.concatenate([points[1].reshape(4 * ROWS, BASIS), jnp.zeros((4 * ROWS, 128 - BASIS), f32)], axis=1),
                jnp.zeros((128 - 4 * ROWS, 128), f32),
            ],
            axis=0,
        ).T[:BASIS, : 4 * ROWS]
    )
    face_at, code_at = slot_rows(dest_ref[...], face_ref[...])

    for r in range(QUANT):
        value = x_ref[r]
        deriv[r] = value
        integral[r] = value

    def degree(k, scale):
        scale = scale / (k + 1)

        def store(q, lanes, value):
            deriv[q, :, lanes] = value
            integral[q, :, lanes] += value * scale

        spatial_products(lambda r: deriv[r], kmat, mixed)
        for tile in range(2):
            spatial_mix(tile, (0, 3, 6), star, mixed, store)
        return scale

    scale = 1.0
    for k in range(1, ORDER):
        scale = degree(k, scale)

    for r in range(QUANT):
        traced = dot(proj[...], split3(integral[r]))
        for f in range(4):
            trace[pl.ds(r * ROWS, ROWS), pl.ds(f * ELEM, ELEM)] = traced[f * ROWS : (f + 1) * ROWS]
    trace[pl.ds(QUANT * ROWS, COMPS - QUANT * ROWS), :] = jnp.zeros((COMPS - QUANT * ROWS, COLS), f32)
    table[...] = split2(trace[...])
    column = iota((COLS, 256), 0)
    slots[...] = halves(dot(table[...], one_hot(column == face_at.astype(jnp.int32))))
    wire = dot(narrow(), split2(slots[...]))
    whole = code_at.astype(jnp.int32)
    partner = jnp.where(whole >= 0, whole + 1 - 2 * (whole % 2), -5).astype(f32)
    at = iota((WIRE, 256), 0)
    wire = jnp.where(at == CODE, code_at, jnp.where(at == PARTNER, partner, wire))
    put_packed(rows, wire[:128].T, jnp.concatenate([wire[128:], wire[128:]], axis=0).T)

    def remote(src, dst, send_sem, recv_sem, device):
        return pltpu.make_async_remote_copy(
            src_ref=src, dst_ref=dst, send_sem=send_sem, recv_sem=recv_sem, device_id=device, device_id_type=MESH
        )

    pl.semaphore_wait(barrier, 31 + 6)
    per = 32 // PIECES

    for i in range(31, 0, -1):
        o, device = peer(i, 1)
        remote(rows.at[o], held.at[member, i], out_send, out_recv.at[i // per], device).start()
    mine = pltpu.make_async_copy(rows.at[own], held.at[member, 0], local_sem)
    mine.start()

    sent = []

    def go(copy):
        copy.start()
        sent.append(copy)

    def part(m, piece):
        return held.at[m, pl.ds(piece * per, per)]

    def ring(m, piece, index, device):
        return remote(part(m, piece), part(m, piece), ring_send.at[index], ring_recv.at[index], device)

    def side(m, piece, index):
        return remote(part(m, piece), part(m, piece), side_send.at[index], side_recv.at[index], to_side)

    def own_piece(piece):
        count = per - 1 if piece == 0 else per
        got = held.at[member, pl.ds(piece * per, count)]
        remote(rows.at[pl.ds(0, count)], got, out_send, out_recv.at[piece], to_up).wait_recv()
        if piece == 0:
            mine.wait()
        go(ring(member, piece, piece, to_up))
        go(ring(member, piece, PIECES + piece, to_down))
        go(side(member, piece, piece))
        if piece in DIRECT:
            go(ring(member, piece, 2 * PIECES + piece, to_far))

    def ring_piece(piece):
        ring(mem_down, piece, piece, to_up).wait_recv()
        if piece % 2 == 0 and piece not in DIRECT:
            go(ring(mem_down, piece, 2 * PIECES + piece, to_up))
        go(side(mem_down, piece, PIECES + piece))
        ring(mem_up, piece, PIECES + piece, to_down).wait_recv()
        if piece % 2 == 1 and piece not in DIRECT:
            go(ring(mem_up, piece, 2 * PIECES + piece, to_down))
        go(side(mem_up, piece, 2 * PIECES + piece))

    def far_piece(piece):
        ring(mem_far, piece, 2 * PIECES + piece, to_up).wait_recv()
        go(side(mem_far, piece, 3 * PIECES + piece))

    def side_pieces(m, index):
        for piece in range(PIECES):
            side(m, piece, index * PIECES + piece).wait_recv()

    def halo_side(s):
        halo_out[s] = halves(dot(table[...], one_hot(column == send_ref[pl.ds(s, 1), :])))

    def own_neighbours(f):
        index = index_ref[pl.ds(f, 1), :]
        raw[:, pl.ds(f * ELEM, ELEM)] = halves(dot(table[...], one_hot(column == index)))

    def face_matrices(f):
        for r in range(QUANT):
            total = normals_ref[0, pl.ds(f, 1), :] * star[0, r]
            for d in range(1, 3):
                total += normals_ref[d, pl.ds(f, 1), :] * star[d, r]
            matrix[f, r] = 0.5 * total

    def keep_volume(q, lanes, value):
        volume[q, :, lanes] = value

    halo_side(0)
    low = remote(halo_out.at[0], halo_in.at[1], halo_send.at[0], halo_recv.at[1], lower)
    low.start()
    halo_side(1)
    high = remote(halo_out.at[1], halo_in.at[0], halo_send.at[1], halo_recv.at[0], upper)
    high.start()
    for i, row in enumerate(friction_params(code_at, region_ref, table_ref)):
        params[pl.ds(i, 1), :] = row
    def wanted():
        return unpacked(held, member)[1][:, PARTNER - 128 : PARTNER - 127]

    def matched(m, want):
        first, second = unpacked(held, m)
        pick = one_hot(want == to_row(second[:, CODE - 128 : CODE - 127]))
        values = jnp.concatenate([first, second], axis=1)
        high_part = values.astype(bf16)
        low_part = (values - high_part.astype(f32)).astype(bf16)
        return dot(pick, high_part) + dot(pick, low_part)

    own_neighbours(0)
    own_piece(0)
    own_neighbours(1)
    own_piece(1)
    own_neighbours(2)
    own_piece(2)
    own_neighbours(3)
    ring_piece(0)
    own_piece(3)
    ring_piece(1)
    want = wanted()
    total = matched(member, want)
    ring_piece(2)
    far_piece(0)
    ring_piece(3)
    total += matched(mem_down, want)
    total += matched(mem_up, want)
    side_pieces(slot(y, 1 - core), 0)
    total += matched(slot(y, 1 - core), want)
    for piece in range(1, PIECES):
        far_piece(piece)
    side_pieces(slot(down, 1 - core), 1)
    total += matched(slot(down, 1 - core), want)
    side_pieces(slot(up, 1 - core), 2)
    total += matched(slot(up, 1 - core), want)
    total += matched(mem_far, want)
    side_pieces(slot(far, 1 - core), 3)
    total += matched(slot(far, 1 - core), want)
    put_packed(replies, total[:, :128], total[:, 128:])

    for i in range(31, 0, -1):
        remote(replies.at[i], back.at[own], back_send, back_recv, peer(i, -1)[1]).start()
    mine = pltpu.make_async_copy(replies.at[0], back.at[own], local_sem)
    mine.start()

    for f in range(4):
        face_matrices(f)
    spatial_products(lambda r: integral[r], kmat, mixed)
    for tile in range(2):
        spatial_mix(tile, (0, 3, 6), star, mixed, keep_volume)

    remote(halo_out.at[1], halo_in.at[0], halo_send.at[1], halo_recv.at[0], upper).wait_recv()
    remote(halo_out.at[0], halo_in.at[1], halo_send.at[0], halo_recv.at[1], lower).wait_recv()
    halo = [split2(halo_in[0]), split2(halo_in[1])]
    first_row = iota((8, ELEM), 0) == 0
    for f in range(4):
        cols = pl.ds(f * ELEM, ELEM)
        index = index_ref[pl.ds(f, 1), :]
        near = dot(halo[0], one_hot(iota((256, ELEM), 0) + COLS == index))
        near += dot(halo[1], one_hot(iota((256, ELEM), 0) + (COLS + 256) == index))
        near = halves(near)
        orient = orient_ref[pl.ds(f, 1), :]
        turn = orient % 3
        reversed_face = orient >= 3
        for r in range(QUANT):
            at = [r * ROWS + 8 * g for g in range(3)]
            group = [raw[pl.ds(a, 8), cols] + near[a : a + 8] for a in at]
            moved = [
                jnp.where(turn == 0, group[g], jnp.where(turn == 1, group[(g + 1) % 3], group[(g + 2) % 3]))
                for g in range(3)
            ]
            for g in range(3):
                reverse = jnp.where(first_row, moved[(3 - g) % 3], flip(moved[(5 - g) % 3]))
                raw[pl.ds(at[g], 8), cols] = jnp.where(reversed_face, reverse, moved[g])
    outer = raw

    for copy in sent:
        copy.wait_send()
    low.wait_send()
    high.wait_send()
    out_done = remote(rows.at[pl.ds(0, 31)], held.at[member, pl.ds(0, 31)], out_send, out_recv.at[0], to_up)
    out_done.wait_send()
    face_col = to_col(face_at).astype(jnp.int32)
    mine.wait()
    returned = remote(replies.at[pl.ds(0, 31)], back.at[pl.ds(0, 31)], back_send, back_recv, to_up)
    returned.wait_send()
    returned.wait_recv()
    first, second = unpacked(back)
    other = dot(widen(), split2(jnp.concatenate([first.T, second.T[: WIRE - 128]], axis=0)))
    law = [params[pl.ds(i, 1), :] for i in range(3)]
    imposed = split2(
        jnp.concatenate(
            [friction(slots[...], other, code_at, law), jnp.zeros((COMPS - QUANT * ROWS, 256), f32)], axis=0
        )
    )

    for f in range(4):
        cols = pl.ds(f * ELEM, ELEM)
        put = face_col == iota((256, ELEM), 1) + f * ELEM
        fault = halves(dot(imposed, one_hot(put)))
        is_fault = jnp.sum(jnp.where(put, 1.0, 0.0), axis=0, keepdims=True) > 0.5
        outer[:, cols] = jnp.where(is_fault, fault, outer[:, cols])
        for tile in range(ELEM // 128):
            lanes = pl.ds(tile * 128, 128)
            cols = pl.ds(f * ELEM + tile * 128, 128)
            speed = 0.5 * speed_ref[:, lanes]
            for chunk in range(3):
                at = [pl.ds(r * ROWS + 8 * chunk, 8) for r in range(QUANT)]
                summed = [trace[at[t], cols] + outer[at[t], cols] for t in range(QUANT)]
                for r in range(QUANT):
                    flux = speed * (trace[at[r], cols] - outer[at[r], cols])
                    for t in range(QUANT):
                        flux += matrix[f, r, pl.ds(t, 1), lanes] * summed[t]
                    fluxes[r, pl.ds(f * ROWS + 8 * chunk, 8), lanes] = flux

    for r in range(QUANT):
        updated_ref[r] = x_ref[r] + 0.25 * (volume[r] - dot(lift[...], split3(fluxes[r])))


def step(*operands):
    vmem, dma = pl.BlockSpec(memory_space=pltpu.VMEM), pltpu.SemaphoreType.DMA
    return pl.pallas_call(
        step_body,
        out_shape=pltpu.VMEM((QUANT, BASIS, ELEM), f32),
        in_specs=[pl.BlockSpec(memory_space=pltpu.HBM)] * 14,
        out_specs=vmem,
        scratch_shapes=[
            pltpu.VMEM((3, QUANT, QUANT, ELEM), f32),
            pltpu.VMEM((3 * BASIS, 3 * BASIS), bf16),
            pltpu.VMEM((4 * ROWS, 3 * BASIS), bf16),
            pltpu.VMEM((BASIS, 12 * ROWS), bf16),
            pltpu.VMEM((QUANT, 3 * BASIS, ELEM), f32),
            pltpu.VMEM((QUANT, BASIS, ELEM), f32),
            pltpu.VMEM((QUANT, BASIS, ELEM), f32),
            pltpu.VMEM((QUANT, BASIS, ELEM), f32),
            pltpu.VMEM((COMPS, COLS), f32),
            pltpu.VMEM((2 * COMPS, COLS), bf16),
            pltpu.VMEM((COMPS, 256), f32),
            pltpu.VMEM((COMPS, COLS), f32),
            pltpu.VMEM((4, QUANT, QUANT, ELEM), f32),
            pltpu.VMEM((QUANT, 4 * ROWS, ELEM), f32),
            pltpu.VMEM((2, 4, ROWS, BASIS), f32),
            pltpu.VMEM((8, 256), f32),
            pltpu.VMEM((32, 12, 128), f32),
            pltpu.VMEM((8, 32, 12, 128), f32),
            pltpu.VMEM((32, 12, 128), f32),
            pltpu.VMEM((32, 12, 128), f32),
            pltpu.VMEM((2, COMPS, 256), f32),
            pltpu.VMEM((2, COMPS, 256), f32),
            dma((2,)), dma((2,)), dma, dma((PIECES,)), dma((3 * PIECES,)), dma((3 * PIECES,)),
            dma((4 * PIECES,)), dma((4 * PIECES,)), dma, dma, dma, dma((14,)),
            *[pltpu.VMEM(o.shape, o.dtype) for o in operands[:13]],
            pltpu.SMEM(operands[13].shape, f32),
        ],
        compiler_params=pltpu.CompilerParams(collective_id=0, has_side_effects=True, vmem_limit_bytes=VMEM_LIMIT),
    )(*operands)


def local(
    element_dofs, star_matrices, face_normals, wave_speed, stiffness, face_projection, face_lift, friction_table,
    neighbour_index, orientation, send_list, fault_face, fault_dest, fault_region,
):
    updated = step(
        jnp.transpose(element_dofs, (1, 0, 2)),
        jnp.transpose(star_matrices, (1, 2, 0, 3)),
        jnp.transpose(stiffness, (1, 0, 2)).reshape(3 * BASIS, BASIS),
        jnp.transpose(face_projection, (1, 0, 2)),
        jnp.transpose(face_lift, (2, 0, 1)),
        face_normals, wave_speed.reshape(1, -1), neighbour_index, orientation, send_list,
        fault_face.reshape(1, -1), fault_dest.reshape(1, -1), fault_region.reshape(1, -1), friction_table,
    )
    return jnp.transpose(updated, (1, 0, 2))


def solution(mesh):
    return jax.shard_map(
        local,
        mesh=mesh,
        in_specs=(
            P(None, None, ("dom", "quad")),
            P(None, None, None, ("dom", "quad")),
            P(None, None, ("dom", "quad")),
            P(("dom", "quad")),
            P(),
            P(),
            P(),
            P(),
            P(None, ("dom", "quad")),
            P(None, ("dom", "quad")),
            P(None, ("dom", "quad")),
            P(("dom", "quad")),
            P(("dom", "quad")),
            P(),
        ),
        out_specs=P(None, None, ("dom", "quad")),
        check_vma=False,
    )
```

```python
import functools
import math

import jax
import jax.numpy as jnp
from jax import lax
from jax.experimental import pallas as pl
from jax.experimental.pallas import tpu as pltpu
from jax.sharding import PartitionSpec as P

ORDER = 6
NEWTON = 8
BASIS = 56
QUANT = 9
ELEM = 256
COLS = 4 * ELEM
ROWS = 24
COMPS = 224
WIRE = 192
CODE, PARTNER = 189, 190
PIECES = 4
DIRECT = (3,)
OFFSETS = [(dz, dx) for dz in (0, 1, 7, 2, 6, 3, 5, 4) for dx in (0, 1, 3, 2)]
f32, bf16 = jnp.float32, jnp.bfloat16
MESH = pl.DeviceIdType.MESH
VMEM_LIMIT = 56 * 1024 * 1024


def iota(shape, dim):
    return lax.broadcasted_iota(jnp.int32, shape, dim)


def one_hot(mask):
    return jnp.where(mask, 1.0, 0.0).astype(bf16)


def split2(x):
    high = x.astype(bf16).astype(f32)
    return jnp.concatenate([high, x - high], axis=0).astype(bf16)


def split3(x):
    high = x.astype(bf16).astype(f32)
    return jnp.concatenate([high, x - high, high], axis=0).astype(bf16)


def dot(a, b):
    return jnp.dot(a, b, preferred_element_type=f32)


def halves(x):
    n = x.shape[0] // 2
    return x[:n] + x[n:]


def to_col(row):
    n = row.shape[1]
    eye = iota((n, n), 0) == iota((n, n), 1)
    return jnp.sum(jnp.where(eye, row, 0.0), axis=1, keepdims=True)


def to_row(col):
    n = col.shape[0]
    eye = iota((n, n), 0) == iota((n, n), 1)
    return jnp.sum(jnp.where(eye, col, 0.0), axis=0, keepdims=True)


def slot_rows(dest, face):
    n = dest.shape[1]
    live = dest >= 0
    owner = jnp.where(live, dest // 1024, 64).astype(f32)
    code = jnp.where(live, dest % 1024, -1).astype(f32)
    owner_col = to_col(owner)
    earlier = (owner_col == owner) & (iota((n, n), 0) < iota((n, n), 1))
    rank = jnp.sum(jnp.where(earlier, 1.0, 0.0), axis=0, keepdims=True)
    place = jnp.where(live, owner * 8.0 + rank, -1.0)
    put = to_col(place) == iota((n, n), 1).astype(f32)
    face_at = jnp.sum(jnp.where(put, to_col(face.astype(f32) + 1.0), 0.0), axis=0, keepdims=True)
    code_at = jnp.sum(jnp.where(put, to_col(code + 1.0), 0.0), axis=0, keepdims=True)
    return face_at - 1.0, code_at - 1.0


def packed(first, second):
    swapped = pltpu.roll(pltpu.roll(second, 64, 1), 252, 0)
    pairs = jnp.where(iota((256, 128), 1) < 64, second, swapped)
    return first.reshape(32, 8, 128), pairs.reshape(32, 8, 128)[:, :4, :]


def put_packed(ref, first, second):
    ref[:, pl.ds(0, 8), :], ref[:, pl.ds(8, 4), :] = packed(first, second)


def unpacked(ref, *at):
    first = ref[(*at, slice(None), pl.ds(0, 8), slice(None))].reshape(256, 128)
    pairs = ref[(*at, slice(None), pl.ds(8, 4), slice(None))]
    pairs = jnp.concatenate([pairs, pairs], axis=1).reshape(256, 128)
    second = jnp.where(iota((256, 128), 0) % 8 < 4, pairs, pltpu.roll(pairs, 64, 1))
    return first, second


def narrow():
    value, row = iota((WIRE, 2 * COMPS), 0), iota((WIRE, 2 * COMPS), 1)
    row = jnp.where(row >= COMPS, row - COMPS, row)
    return one_hot((row == value + ((value * 9363) >> 16)) & (value < CODE))


def widen():
    row, value = iota((COMPS, 2 * WIRE), 0), iota((COMPS, 2 * WIRE), 1)
    value = jnp.where(value >= WIRE, value - WIRE, value)
    return one_hot((row == value + ((value * 9363) >> 16)) & (value < CODE))


def weight_parts(weights):
    high = weights.astype(bf16).astype(f32)
    return jnp.concatenate([high, high, weights - high], axis=1).astype(bf16)


def spatial_products(load, kmat_ref, mixed):
    for r in range(QUANT):
        mixed[r] = dot(kmat_ref[...], split3(load(r)))


def spatial_mix(tile, firsts, star_ref, mixed, store):
    lanes = pl.ds(tile * 128, 128)
    for first in firsts:
        total = [None] * 3
        for d in range(3):
            for r in range(QUANT):
                value = mixed[r, pl.ds(d * BASIS, BASIS), lanes]
                for i in range(3):
                    term = star_ref[d, first + i, pl.ds(r, 1), lanes] * value
                    total[i] = term if total[i] is None else total[i] + term
        for i in range(3):
            store(first + i, lanes, total[i])


def friction_params(code_at, region_ref, table_ref):
    code_col = to_col(code_at).astype(jnp.int32)
    pairs = region_ref.shape[1] // 32
    regions = jnp.concatenate(
        [jnp.broadcast_to(region_ref[:, pl.ds(o * pairs, pairs)], (8, pairs)) for o in range(32)], axis=0
    ).astype(f32)
    hit = (code_col // 2 == iota((256, pairs), 1)) & (code_col >= 0)
    region = to_row(jnp.sum(jnp.where(hit, regions, 0.0), axis=1, keepdims=True))
    params = []
    for row in range(3):
        value = jnp.full((1, 256), table_ref[row, 0], f32)
        for j in range(1, 8):
            value = jnp.where(region == float(j), table_ref[row, j], value)
        params.append(value)
    return params


def friction(own, other, code_at, params):
    rate_term, state_term, shear = params
    background = 3.0 * shear

    def comp(x, r):
        return x[r * ROWS : (r + 1) * ROWS]

    second = (code_at.astype(jnp.int32) % 2) == 1
    sign = jnp.where(second, -1.0, 1.0)
    pressure = 1.0 + jax.nn.softplus(2.0 - 0.5 * (comp(own, 0) + comp(other, 0)))
    locked = (
        0.5 * (comp(own, 3) + comp(other, 3)) + 0.5 * sign * (comp(other, 7) - comp(own, 7)) + background
    )
    stiff_rate = 0.5 * jnp.exp(state_term / rate_term)
    slip = jnp.zeros_like(locked)
    for _ in range(NEWTON):
        argument = stiff_rate * slip
        root = jnp.sqrt(1.0 + argument * argument)
        arsinh = jnp.log(jnp.abs(argument) + root)
        mismatch = 0.5 * slip + pressure * rate_term * jnp.where(argument < 0.0, -arsinh, arsinh) - locked
        gradient = 0.5 + pressure * rate_term * stiff_rate / root
        slip = slip - 0.4 * mismatch / gradient
    third = 2.0 * (locked - 0.5 * slip - background) - comp(own, 3)
    seventh = comp(other, 7) - sign * slip
    return jnp.concatenate(
        [other[: 3 * ROWS], third, other[4 * ROWS : 7 * ROWS], seventh, other[8 * ROWS : QUANT * ROWS]], axis=0
    )


def flip(x):
    index = 7 - iota((8, 128), 0)
    parts = [
        jnp.take_along_axis(x[:, c : c + 128], index, axis=0, mode="promise_in_bounds") for c in range(0, x.shape[1], 128)
    ]
    return jnp.concatenate(parts, axis=1)


def step_body(*refs):
    sources, refs = refs[:14], refs[14:]
    copied, refs = refs[-14:], refs[:-14]
    (
        x_ref, star_in, stiff_ref, proj_in, lift_in, normals_ref, speed_ref, index_ref,
        orient_ref, send_ref, face_ref, dest_ref, region_ref, table_ref,
    ) = copied
    (
        updated_ref,
        star, kmat, proj, lift, mixed, deriv, integral, volume, trace, table, slots, raw, matrix, fluxes, points, params,
        rows, held, replies, back, halo_out, halo_in, placed,
        halo_send, halo_recv, out_send, out_recv, ring_send, ring_recv, side_send, side_recv, back_send, back_recv, local_sem, in_sem,
    ) = refs
    dom, quad = lax.axis_index("dom"), lax.axis_index("quad")
    doms = lax.axis_size("dom")
    block, member = dom // 8, dom % 8
    y, core = member // 2, member % 2
    own = block * 4 + quad

    def slot(yy, cc):
        return yy * 2 + cc

    def peer(i, sign):
        dz, dx = OFFSETS[i]
        zz, xx = lax.rem(block + (8 + sign * dz) % 8, 8), lax.rem(quad + (4 + sign * dx) % 4, 4)
        return zz * 4 + xx, (zz * 8 + member, xx)

    up, down, far = (y + 1) % 4, (y + 3) % 4, (y + 2) % 4
    mem_up, mem_down, mem_far = slot(up, core), slot(down, core), slot(far, core)
    to_up, to_down = (block * 8 + mem_up, quad), (block * 8 + mem_down, quad)
    to_far = (block * 8 + mem_far, quad)
    to_side = (block * 8 + slot(y, 1 - core), quad)
    upper, lower = (lax.rem(dom + 1, doms), quad), (lax.rem(dom + doms - 1, doms), quad)

    arriving = [pltpu.make_async_copy(source, held_in, in_sem.at[i]) for i, (source, held_in) in enumerate(zip(sources, copied))]
    for copy in arriving:
        copy.start()

    barrier = pltpu.get_barrier_semaphore()

    for i in range(31, 0, -1):
        pl.semaphore_signal(barrier, inc=1, device_id=peer(i, -1)[1], device_id_type=MESH)
    for device in (to_up, to_down, to_side, to_far, upper, lower):
        pl.semaphore_signal(barrier, inc=1, device_id=device, device_id_type=MESH)

    for copy in arriving:
        copy.wait()
    for q in range(QUANT):
        for r in range(QUANT):
            star[:, q, r, :] = star_in[q, r]
    kmat[...] = weight_parts(stiff_ref[...])
    for source, padded in ((proj_in, points.at[0]), (lift_in, points.at[1])):
        padded[...] = jnp.zeros_like(padded)
        for p in range(21):
            padded[:, p // 7 * 8 + p % 7, :] = source[p]
    proj[...] = weight_parts(points[0].reshape(4 * ROWS, BASIS))
    turned = jnp.concatenate(
        [
            jnp.concatenate([points[1].reshape(4 * ROWS, BASIS), jnp.zeros((4 * ROWS, 128 - BASIS), f32)], axis=1),
            jnp.zeros((128 - 4 * ROWS, 128), f32),
        ],
        axis=0,
    ).T[:BASIS, : 4 * ROWS]
    turned_high = turned.astype(bf16).astype(f32)
    lift[...] = jnp.concatenate(
        [
            jnp.concatenate([turned_high, turned_high], axis=1),
            jnp.concatenate([turned - turned_high, jnp.zeros((BASIS, 4 * ROWS), f32)], axis=1),
        ],
        axis=0,
    ).astype(bf16)
    face_at, code_at = slot_rows(dest_ref[...], face_ref[...])

    for r in range(QUANT):
        value = x_ref[r]
        deriv[r] = value
        integral[r] = value

    def degree(k, scale):
        scale = scale / (k + 1)

        def store(q, lanes, value):
            deriv[q, :, lanes] = value
            integral[q, :, lanes] += value * scale

        spatial_products(lambda r: deriv[r], kmat, mixed)
        for tile in range(2):
            spatial_mix(tile, (0, 3, 6), star, mixed, store)
        return scale

    scale = 1.0
    for k in range(1, ORDER):
        scale = degree(k, scale)

    for r in range(QUANT):
        traced = dot(proj[...], split3(integral[r]))
        for f in range(4):
            trace[pl.ds(r * ROWS, ROWS), pl.ds(f * ELEM, ELEM)] = traced[f * ROWS : (f + 1) * ROWS]
    trace[pl.ds(QUANT * ROWS, COMPS - QUANT * ROWS), :] = jnp.zeros((COMPS - QUANT * ROWS, COLS), f32)
    table[...] = split2(trace[...])
    column = iota((COLS, 256), 0)
    slots[...] = halves(dot(table[...], one_hot(column == face_at.astype(jnp.int32))))
    wire = dot(narrow(), split2(slots[...]))
    whole = code_at.astype(jnp.int32)
    partner = jnp.where(whole >= 0, whole + 1 - 2 * (whole % 2), -5).astype(f32)
    at = iota((WIRE, 256), 0)
    wire = jnp.where(at == CODE, code_at, jnp.where(at == PARTNER, partner, wire))
    put_packed(rows, wire[:128].T, jnp.concatenate([wire[128:], wire[128:]], axis=0).T)

    def remote(src, dst, send_sem, recv_sem, device):
        return pltpu.make_async_remote_copy(
            src_ref=src, dst_ref=dst, send_sem=send_sem, recv_sem=recv_sem, device_id=device, device_id_type=MESH
        )

    pl.semaphore_wait(barrier, 31 + 6)
    per = 32 // PIECES

    for i in range(31, 0, -1):
        o, device = peer(i, 1)
        remote(rows.at[o], held.at[member, i], out_send, out_recv.at[i // per], device).start()
    mine = pltpu.make_async_copy(rows.at[own], held.at[member, 0], local_sem)
    mine.start()

    sent = []

    def go(copy):
        copy.start()
        sent.append(copy)

    def part(m, piece):
        return held.at[m, pl.ds(piece * per, per)]

    def ring(m, piece, index, device):
        return remote(part(m, piece), part(m, piece), ring_send.at[index], ring_recv.at[index], device)

    def side(m, piece, index):
        return remote(part(m, piece), part(m, piece), side_send.at[index], side_recv.at[index], to_side)

    def own_piece(piece):
        count = per - 1 if piece == 0 else per
        got = held.at[member, pl.ds(piece * per, count)]
        remote(rows.at[pl.ds(0, count)], got, out_send, out_recv.at[piece], to_up).wait_recv()
        if piece == 0:
            mine.wait()
        go(ring(member, piece, piece, to_up))
        go(ring(member, piece, PIECES + piece, to_down))
        go(side(member, piece, piece))
        if piece in DIRECT:
            go(ring(member, piece, 2 * PIECES + piece, to_far))

    def ring_piece(piece):
        ring(mem_down, piece, piece, to_up).wait_recv()
        if piece % 2 == 0 and piece not in DIRECT:
            go(ring(mem_down, piece, 2 * PIECES + piece, to_up))
        go(side(mem_down, piece, PIECES + piece))
        ring(mem_up, piece, PIECES + piece, to_down).wait_recv()
        if piece % 2 == 1 and piece not in DIRECT:
            go(ring(mem_up, piece, 2 * PIECES + piece, to_down))
        go(side(mem_up, piece, 2 * PIECES + piece))

    def far_piece(piece):
        ring(mem_far, piece, 2 * PIECES + piece, to_up).wait_recv()
        go(side(mem_far, piece, 3 * PIECES + piece))

    def side_pieces(m, index):
        for piece in range(PIECES):
            side(m, piece, index * PIECES + piece).wait_recv()

    def halo_side(s):
        halo_out[s] = halves(dot(table[...], one_hot(column == send_ref[pl.ds(s, 1), :])))

    def own_neighbours(f):
        index = index_ref[pl.ds(f, 1), :]
        raw[:, pl.ds(f * ELEM, ELEM)] = halves(dot(table[...], one_hot(column == index)))

    def face_matrices(f):
        for r in range(QUANT):
            total = normals_ref[0, pl.ds(f, 1), :] * star[0, r]
            for d in range(1, 3):
                total += normals_ref[d, pl.ds(f, 1), :] * star[d, r]
            matrix[f, r] = 0.5 * total

    def keep_volume(q, lanes, value):
        volume[q, :, lanes] = value

    halo_side(0)
    low = remote(halo_out.at[0], halo_in.at[1], halo_send.at[0], halo_recv.at[1], lower)
    low.start()
    halo_side(1)
    high = remote(halo_out.at[1], halo_in.at[0], halo_send.at[1], halo_recv.at[0], upper)
    high.start()
    for i, row in enumerate(friction_params(code_at, region_ref, table_ref)):
        params[pl.ds(i, 1), :] = row
    def wanted():
        return unpacked(held, member)[1][:, PARTNER - 128 : PARTNER - 127]

    def matched(m, want):
        first, second = unpacked(held, m)
        pick = one_hot(want == to_row(second[:, CODE - 128 : CODE - 127]))
        values = jnp.concatenate([first, second], axis=1)
        high_part = values.astype(bf16)
        low_part = (values - high_part.astype(f32)).astype(bf16)
        return dot(pick, high_part) + dot(pick, low_part)

    own_neighbours(0)
    own_piece(0)
    own_neighbours(1)
    own_piece(1)
    own_neighbours(2)
    own_piece(2)
    own_neighbours(3)
    ring_piece(0)
    own_piece(3)
    ring_piece(1)
    want = wanted()
    total = matched(member, want)
    ring_piece(2)
    far_piece(0)
    ring_piece(3)
    total += matched(mem_down, want)
    far_piece(1)
    far_piece(3)
    total += matched(mem_up, want)
    far_piece(2)
    for i, m in enumerate((slot(y, 1 - core), slot(down, 1 - core), slot(up, 1 - core))):
        side_pieces(m, i)
        total += matched(m, want)
    total += matched(mem_far, want)
    side_pieces(slot(far, 1 - core), 3)
    total += matched(slot(far, 1 - core), want)
    put_packed(replies, total[:, :128], total[:, 128:])

    for i in range(31, 0, -1):
        remote(replies.at[i], back.at[own], back_send, back_recv, peer(i, -1)[1]).start()
    mine = pltpu.make_async_copy(replies.at[0], back.at[own], local_sem)
    mine.start()

    for f in range(4):
        face_matrices(f)
    spatial_products(lambda r: integral[r], kmat, mixed)
    for tile in range(2):
        spatial_mix(tile, (0, 3, 6), star, mixed, keep_volume)

    remote(halo_out.at[1], halo_in.at[0], halo_send.at[1], halo_recv.at[0], upper).wait_recv()
    remote(halo_out.at[0], halo_in.at[1], halo_send.at[0], halo_recv.at[1], lower).wait_recv()
    halo = [split2(halo_in[0]), split2(halo_in[1])]
    first_row = iota((8, ELEM), 0) == 0
    for f in range(4):
        cols = pl.ds(f * ELEM, ELEM)
        index = index_ref[pl.ds(f, 1), :]
        near = dot(halo[0], one_hot(iota((256, ELEM), 0) + COLS == index))
        near += dot(halo[1], one_hot(iota((256, ELEM), 0) + (COLS + 256) == index))
        near = halves(near)
        orient = orient_ref[pl.ds(f, 1), :]
        turn = orient % 3
        reversed_face = orient >= 3
        for r in range(QUANT):
            at = [r * ROWS + 8 * g for g in range(3)]
            group = [raw[pl.ds(a, 8), cols] + near[a : a + 8] for a in at]
            moved = [
                jnp.where(turn == 0, group[g], jnp.where(turn == 1, group[(g + 1) % 3], group[(g + 2) % 3]))
                for g in range(3)
            ]
            for g in range(3):
                reverse = jnp.where(first_row, moved[(3 - g) % 3], flip(moved[(5 - g) % 3]))
                raw[pl.ds(at[g], 8), cols] = jnp.where(reversed_face, reverse, moved[g])
    outer = raw

    for copy in sent:
        copy.wait_send()
    low.wait_send()
    high.wait_send()
    out_done = remote(rows.at[pl.ds(0, 31)], held.at[member, pl.ds(0, 31)], out_send, out_recv.at[0], to_up)
    out_done.wait_send()
    face_col = to_col(face_at).astype(jnp.int32)
    for f in range(4):
        cols = pl.ds(f * ELEM, ELEM)
        put = face_col == iota((256, ELEM), 1) + f * ELEM
        placed[:, cols] = one_hot(put)
        is_fault = jnp.sum(jnp.where(put, 1.0, 0.0), axis=0, keepdims=True) > 0.5
        outer[:, cols] = jnp.where(is_fault, 0.0, outer[:, cols])
    widening = widen()
    mine.wait()
    returned = remote(replies.at[pl.ds(0, 31)], back.at[pl.ds(0, 31)], back_send, back_recv, to_up)
    returned.wait_send()
    returned.wait_recv()
    first, second = unpacked(back)
    other = dot(widening, split2(jnp.concatenate([first.T, second.T[: WIRE - 128]], axis=0)))
    law = [params[pl.ds(i, 1), :] for i in range(3)]
    imposed = split2(
        jnp.concatenate(
            [friction(slots[...], other, code_at, law), jnp.zeros((COMPS - QUANT * ROWS, 256), f32)], axis=0
        )
    )

    for f in range(4):
        cols = pl.ds(f * ELEM, ELEM)
        outer[:, cols] += halves(dot(imposed, placed[:, cols]))
        for tile in range(ELEM // 128):
            lanes = pl.ds(tile * 128, 128)
            cols = pl.ds(f * ELEM + tile * 128, 128)
            speed = 0.5 * speed_ref[:, lanes]
            for chunk in range(3):
                at = [pl.ds(r * ROWS + 8 * chunk, 8) for r in range(QUANT)]
                summed = [trace[at[t], cols] + outer[at[t], cols] for t in range(QUANT)]
                for r in range(QUANT):
                    flux = speed * (trace[at[r], cols] - outer[at[r], cols])
                    for t in range(QUANT):
                        flux += matrix[f, r, pl.ds(t, 1), lanes] * summed[t]
                    fluxes[r, pl.ds(f * ROWS + 8 * chunk, 8), lanes] = flux

    for r in range(QUANT):
        updated_ref[r] = x_ref[r] + 0.25 * (volume[r] - halves(dot(lift[...], split2(fluxes[r]))))


def step(*operands):
    vmem, dma = pl.BlockSpec(memory_space=pltpu.VMEM), pltpu.SemaphoreType.DMA
    return pl.pallas_call(
        step_body,
        out_shape=pltpu.VMEM((QUANT, BASIS, ELEM), f32),
        in_specs=[pl.BlockSpec(memory_space=pltpu.HBM)] * 14,
        out_specs=vmem,
        scratch_shapes=[
            pltpu.VMEM((3, QUANT, QUANT, ELEM), f32),
            pltpu.VMEM((3 * BASIS, 3 * BASIS), bf16),
            pltpu.VMEM((4 * ROWS, 3 * BASIS), bf16),
            pltpu.VMEM((2 * BASIS, 8 * ROWS), bf16),
            pltpu.VMEM((QUANT, 3 * BASIS, ELEM), f32),
            pltpu.VMEM((QUANT, BASIS, ELEM), f32),
            pltpu.VMEM((QUANT, BASIS, ELEM), f32),
            pltpu.VMEM((QUANT, BASIS, ELEM), f32),
            pltpu.VMEM((COMPS, COLS), f32),
            pltpu.VMEM((2 * COMPS, COLS), bf16),
            pltpu.VMEM((COMPS, 256), f32),
            pltpu.VMEM((COMPS, COLS), f32),
            pltpu.VMEM((4, QUANT, QUANT, ELEM), f32),
            pltpu.VMEM((QUANT, 4 * ROWS, ELEM), f32),
            pltpu.VMEM((2, 4, ROWS, BASIS), f32),
            pltpu.VMEM((8, 256), f32),
            pltpu.VMEM((32, 12, 128), f32),
            pltpu.VMEM((8, 32, 12, 128), f32),
            pltpu.VMEM((32, 12, 128), f32),
            pltpu.VMEM((32, 12, 128), f32),
            pltpu.VMEM((2, COMPS, 256), f32),
            pltpu.VMEM((2, COMPS, 256), f32),
            pltpu.VMEM((256, COLS), bf16),
            dma((2,)), dma((2,)), dma, dma((PIECES,)), dma((3 * PIECES,)), dma((3 * PIECES,)),
            dma((4 * PIECES,)), dma((4 * PIECES,)), dma, dma, dma, dma((14,)),
            *[pltpu.VMEM(o.shape, o.dtype) for o in operands[:13]],
            pltpu.SMEM(operands[13].shape, f32),
        ],
        compiler_params=pltpu.CompilerParams(collective_id=0, has_side_effects=True, vmem_limit_bytes=VMEM_LIMIT),
    )(*operands)


def local(
    element_dofs, star_matrices, face_normals, wave_speed, stiffness, face_projection, face_lift, friction_table,
    neighbour_index, orientation, send_list, fault_face, fault_dest, fault_region,
):
    updated = step(
        jnp.transpose(element_dofs, (1, 0, 2)),
        jnp.transpose(star_matrices, (1, 2, 0, 3)),
        jnp.transpose(stiffness, (1, 0, 2)).reshape(3 * BASIS, BASIS),
        jnp.transpose(face_projection, (1, 0, 2)),
        jnp.transpose(face_lift, (2, 0, 1)),
        face_normals, wave_speed.reshape(1, -1), neighbour_index, orientation, send_list,
        fault_face.reshape(1, -1), fault_dest.reshape(1, -1), fault_region.reshape(1, -1), friction_table,
    )
    return jnp.transpose(updated, (1, 0, 2))


def solution(mesh):
    return jax.shard_map(
        local,
        mesh=mesh,
        in_specs=(
            P(None, None, ("dom", "quad")),
            P(None, None, None, ("dom", "quad")),
            P(None, None, ("dom", "quad")),
            P(("dom", "quad")),
            P(),
            P(),
            P(),
            P(),
            P(None, ("dom", "quad")),
            P(None, ("dom", "quad")),
            P(None, ("dom", "quad")),
            P(("dom", "quad")),
            P(("dom", "quad")),
            P(),
        ),
        out_specs=P(None, None, ("dom", "quad")),
        check_vma=False,
    )
```
